512 devices in a mesh: blk: 32 (over z_lo, y, core), space: 16 (over x, z_hi).
Axes of the slice: x: 4, y: 8, z: 8 (z_hi: 4, z_lo: 2; z = z_hi * 2 + z_lo), core: 2. Of those that a mesh axis runs over, the one named last changes fastest.
Arguments:
- input_field: bfloat16 [128, 96, 96, 192], P('blk', 'space'), may hold values from -6 to 6
- cotangent: bfloat16 [128, 96, 96, 192], P('blk', 'space'), may hold values from -0.59765625 to 0.59765625
- weights: bfloat16 [16, 32, 8, 2, 128, 128], P('space', 'blk'), may hold values from -0.375 to 0.375
Outputs:
- spectral_out: bfloat16 [128, 96, 96, 192], P('blk', 'space')
- field_grad: bfloat16 [128, 96, 96, 192], P('blk', 'space')
- weight_grad: float32 [16, 32, 8, 2, 128, 128], P('space', 'blk')
The draws below stay inside these ranges and needn't reach their ends.
All inputs are finite; a program needn't handle non-finite values.
Results may differ from the reference program's by a relative error of at most 0.015.
Values may be sent and summed in bfloat16 or wider, within the bound.
No kernel may reach another device: no remote copies, remote signals or barrier semaphores. Data moves between devices by JAX's collectives and lax.ppermute only.
A program may use at most 64 MiB of HBM per device.

```python
import math
import jax
import jax.numpy as jnp
from jax import lax

C = 128
NX = 96
NY = 192
NZ = 96
MX = 16
MY = 32
MZ = 8


def block_scale(own_key, dims, pieces, smallest, high):
    factor_of = 1.0
    for dim, blocks in pieces:
        draws = jax.random.uniform(jax.random.fold_in(jax.random.fold_in(own_key, 6), dim), (blocks,), jnp.float32, smallest / len(pieces), high / len(pieces))
        factor_of = factor_of * jnp.repeat(jnp.exp(draws), dims[dim] // blocks).reshape((-1,) + (1,) * (len(dims) - 1 - dim))
    return factor_of


def scatter_about(own_key, extent, spread, most, pieces=(), held_as=jnp.bfloat16):
    result = spread * jax.random.normal(own_key, extent, jnp.float32)
    if pieces:
        result = result * block_scale(own_key, extent, pieces, -0.22, 0.18)
    return jnp.clip(result, -most, most).astype(held_as)


def setup_inputs(seed: int = 0) -> dict:
    keys = jax.random.split(jax.random.key(seed), 4)
    return {
        "input_field": scatter_about(keys[0], (C, NZ, NX, NY), 1.0, 6.0, ((0, 32), (1, 16))),
        "cotangent": scatter_about(keys[1], (C, NZ, NX, NY), 0.1, 0.59765625, ((0, 32), (1, 16))),
        "weights": scatter_about(keys[2], (MX, MY, MZ, 2, C, C), (2 * C) ** -0.5, 0.375, ((0, 16), (1, 32))),
    }


def centered_freqs(total_count):
    indices = jnp.arange(total_count, dtype=jnp.int32)
    return jnp.where(indices < total_count // 2, indices, indices - total_count)

def phase_pair(frequencies, positions, length):
    product = frequencies[:, None] * positions[None, :] % length
    angles = product.astype(jnp.float32) * (2.0 * math.pi / length)
    return (jnp.cos(angles), jnp.sin(angles))

def x_analysis_table():
    cosines, sine_values = phase_pair(centered_freqs(MX), jnp.arange(NX, dtype=jnp.int32), NX)
    return jnp.stack([cosines.T, -sine_values.T], 1).astype(jnp.bfloat16)

def y_analysis_table():
    cosines, sine_values = phase_pair(centered_freqs(MY), jnp.arange(NY, dtype=jnp.int32), NY)
    real_rows = jnp.stack([cosines.T, -sine_values.T], 1)
    imag_rows = jnp.stack([sine_values.T, cosines.T], 1)
    return jnp.stack([real_rows, imag_rows], 0).astype(jnp.bfloat16)

def z_analysis_table(positions):
    cosines, sine_values = phase_pair(jnp.arange(MZ, dtype=jnp.int32), positions, NZ)
    real_rows = jnp.stack([cosines.T, -sine_values.T], 1)
    imag_rows = jnp.stack([sine_values.T, cosines.T], 1)
    return jnp.stack([real_rows, imag_rows], 0).astype(jnp.bfloat16)

def mode_weights():
    return jnp.where(jnp.arange(MZ) == 0, 1.0, 2.0).astype(jnp.float32)

def z_synthesis_table(positions, amplitude):
    cosines, sine_values = phase_pair(jnp.arange(MZ, dtype=jnp.int32), positions, NZ)
    cosines = cosines * amplitude[:, None]
    sine_values = sine_values * amplitude[:, None]
    real_rows = jnp.stack([cosines, sine_values], -1)
    imag_rows = jnp.stack([-sine_values, cosines], -1)
    return jnp.stack([real_rows, imag_rows], 1).astype(jnp.bfloat16)

def y_synthesis_table():
    cosines, sine_values = phase_pair(centered_freqs(MY), jnp.arange(NY, dtype=jnp.int32), NY)
    real_rows = jnp.stack([cosines, sine_values], 1)
    imag_rows = jnp.stack([-sine_values, cosines], 1)
    return jnp.stack([real_rows, imag_rows], 0).astype(jnp.bfloat16)

def x_synthesis_table():
    cosines, sine_values = phase_pair(centered_freqs(MX), jnp.arange(NX, dtype=jnp.int32), NX)
    return jnp.stack([cosines, -sine_values], 0).astype(jnp.bfloat16)

def contract(pattern, first_operand, second_operand):
    return jnp.einsum(pattern, first_operand.astype(jnp.float32), second_operand.astype(jnp.float32), precision=lax.Precision.HIGHEST)

def analyse(values, x_table, y_table):

    def one_group(channel_block):
        xsum = contract('czxy,xrp->czrpy', channel_block, x_table).astype(jnp.bfloat16)
        return contract('czrpy,ryoq->czopq', xsum, y_table).astype(jnp.bfloat16)
    groups = values.reshape(C // 8, 8, NZ, NX, NY)
    return lax.map(one_group, groups).reshape(C, NZ, 2, MX, MY)

def synthesize(zback, y_table, x_table):

    def one_group(channel_block):
        yback = contract('czipq,iqoy->czopy', channel_block, y_table).astype(jnp.bfloat16)
        return contract('czipy,ipx->czxy', yback, x_table).astype(jnp.bfloat16)
    groups = zback.reshape(C // 8, 8, NZ, 2, MX, MY)
    return lax.map(one_group, groups).reshape(C, NZ, NX, NY)

def reference(input_field, cotangent, weights):
    forward_scale = 1.0 / math.sqrt(NX * NY * NZ)
    synth_scale = 1.0 / math.sqrt(MX * MY * MZ)
    amplitude = mode_weights()
    x_table = x_analysis_table()
    y_table = y_analysis_table()
    plane_f = analyse(input_field, x_table, y_table)
    plane_g = analyse(cotangent, x_table, y_table)
    z_positions = jnp.arange(NZ, dtype=jnp.int32)
    z_table = z_analysis_table(z_positions)
    zsum_f = contract('czipq,izok->ckopq', plane_f, z_table)
    zsum_g = contract('czipq,izok->ckopq', plane_g, z_table)
    spec_f = (zsum_f * forward_scale).astype(jnp.bfloat16)
    spec_g = (zsum_g * (amplitude * synth_scale)[None, :, None, None, None]).astype(jnp.bfloat16)
    w_real = weights[:, :, :, 0]
    w_imag = weights[:, :, :, 1]
    f_real = spec_f[:, :, 0]
    f_imag = spec_f[:, :, 1]
    g_real = spec_g[:, :, 0]
    g_imag = spec_g[:, :, 1]
    mixed_real = contract('abkoc,ckab->okab', w_real, f_real) - contract('abkoc,ckab->okab', w_imag, f_imag)
    mixed_imag = contract('abkoc,ckab->okab', w_real, f_imag) + contract('abkoc,ckab->okab', w_imag, f_real)
    mixed = jnp.stack([mixed_real, mixed_imag], 2).astype(jnp.bfloat16)
    grad_real = contract('abkoc,okab->ckab', w_real, g_real) + contract('abkoc,okab->ckab', w_imag, g_imag)
    grad_imag = contract('abkoc,okab->ckab', w_real, g_imag) - contract('abkoc,okab->ckab', w_imag, g_real)
    grad_spec = jnp.stack([grad_real, grad_imag], 2).astype(jnp.bfloat16)
    wgrad_real = contract('okab,ckab->abkoc', g_real, f_real) + contract('okab,ckab->abkoc', g_imag, f_imag)
    wgrad_imag = contract('okab,ckab->abkoc', g_imag, f_real) - contract('okab,ckab->abkoc', g_real, f_imag)
    weight_grad = jnp.stack([wgrad_real, wgrad_imag], 3)
    unit_weights = jnp.ones((MZ,), jnp.float32)
    zback_y = (contract('ckipq,kizo->czopq', mixed, z_synthesis_table(z_positions, amplitude)) * synth_scale).astype(jnp.bfloat16)
    zback_u = (contract('ckipq,kizo->czopq', grad_spec, z_synthesis_table(z_positions, unit_weights)) * forward_scale).astype(jnp.bfloat16)
    y_back_table = y_synthesis_table()
    x_back_table = x_synthesis_table()
    spectral_out = synthesize(zback_y, y_back_table, x_back_table)
    field_grad = synthesize(zback_u, y_back_table, x_back_table)
    return (spectral_out, field_grad, weight_grad)
```

```python
import math

import jax
import jax.numpy as jnp
from jax import lax
from jax.sharding import PartitionSpec as P

NX = 96
NY = 192
NZ = 96
MX = 16
MY = 32
MZ = 8


def centered_freqs(total_count):
    indices = jnp.arange(total_count, dtype=jnp.int32)
    return jnp.where(indices < total_count // 2, indices, indices - total_count)


def phase_pair(frequencies, positions, length):
    product = frequencies[:, None] * positions[None, :] % length
    angles = product.astype(jnp.float32) * (2.0 * math.pi / length)
    return (jnp.cos(angles), jnp.sin(angles))


def x_analysis_table():
    cosines, sine_values = phase_pair(centered_freqs(MX), jnp.arange(NX, dtype=jnp.int32), NX)
    return jnp.stack([cosines.T, -sine_values.T], 1).astype(jnp.bfloat16)


def y_analysis_table():
    cosines, sine_values = phase_pair(centered_freqs(MY), jnp.arange(NY, dtype=jnp.int32), NY)
    real_rows = jnp.stack([cosines.T, -sine_values.T], 1)
    imag_rows = jnp.stack([sine_values.T, cosines.T], 1)
    return jnp.stack([real_rows, imag_rows], 0).astype(jnp.bfloat16)


def z_analysis_table(positions):
    cosines, sine_values = phase_pair(jnp.arange(MZ, dtype=jnp.int32), positions, NZ)
    real_rows = jnp.stack([cosines.T, -sine_values.T], 1)
    imag_rows = jnp.stack([sine_values.T, cosines.T], 1)
    return jnp.stack([real_rows, imag_rows], 0).astype(jnp.bfloat16)


def mode_weights():
    return jnp.where(jnp.arange(MZ) == 0, 1.0, 2.0).astype(jnp.float32)


def z_synthesis_table(positions, amplitude):
    cosines, sine_values = phase_pair(jnp.arange(MZ, dtype=jnp.int32), positions, NZ)
    cosines = cosines * amplitude[:, None]
    sine_values = sine_values * amplitude[:, None]
    real_rows = jnp.stack([cosines, sine_values], -1)
    imag_rows = jnp.stack([-sine_values, cosines], -1)
    return jnp.stack([real_rows, imag_rows], 1).astype(jnp.bfloat16)


def y_synthesis_table():
    cosines, sine_values = phase_pair(centered_freqs(MY), jnp.arange(NY, dtype=jnp.int32), NY)
    real_rows = jnp.stack([cosines, sine_values], 1)
    imag_rows = jnp.stack([-sine_values, cosines], 1)
    return jnp.stack([real_rows, imag_rows], 0).astype(jnp.bfloat16)


def x_synthesis_table():
    cosines, sine_values = phase_pair(centered_freqs(MX), jnp.arange(NX, dtype=jnp.int32), NX)
    return jnp.stack([cosines, -sine_values], 0).astype(jnp.bfloat16)


def contract(pattern, first_operand, second_operand):
    return jnp.einsum(pattern, first_operand, second_operand, preferred_element_type=jnp.float32)


def shards(input_field, cotangent, weights):
    forward_scale = 1.0 / math.sqrt(NX * NY * NZ)
    synth_scale = 1.0 / math.sqrt(MX * MY * MZ)
    amplitude = mode_weights()
    unit_weights = jnp.ones((MZ,), jnp.float32)
    n_space = lax.axis_size("space")
    n_blk = lax.axis_size("blk")
    chans, cells = input_field.shape[:2]
    x_table = x_analysis_table()
    y_table = y_analysis_table()

    def analyse(values):
        xsum = contract("czxy,xrp->czrpy", values, x_table).astype(jnp.bfloat16)
        return contract("czrpy,ryoq->pczoq", xsum, y_table).astype(jnp.bfloat16)

    planes = jnp.stack([analyse(input_field), analyse(cotangent)], 3)
    planes = planes.reshape(n_space, chans * cells, 2 * 2 * MY)
    planes = lax.all_to_all(planes, "space", 0, 0, tiled=True)
    planes = planes.reshape(n_space, chans, cells, 2, 2, MY)
    z_table = z_analysis_table(jnp.arange(NZ, dtype=jnp.int32))
    z_table = z_table.reshape(2, n_space, cells, 2, MZ)
    zsum = contract("sczhiq,iszok->qhcko", planes, z_table)
    scales = jnp.stack([jnp.full((MZ,), forward_scale, jnp.float32), amplitude * synth_scale])
    spec = (zsum * scales[None, :, None, :, None]).astype(jnp.bfloat16)
    spec = spec.reshape(n_blk, 1, 2 * chans * MZ * 2)
    spec = lax.all_to_all(spec, "blk", 0, 0, tiled=True)
    spec = spec.reshape(n_blk, 2, chans, MZ, 2).transpose(1, 4, 3, 0, 2).reshape(2, 2, MZ, n_blk * chans)
    f_real, f_imag = spec[0, 0], spec[0, 1]
    g_real, g_imag = spec[1, 0], spec[1, 1]
    w_real = weights[0, 0, :, 0]
    w_imag = weights[0, 0, :, 1]
    mixed_real = contract("koc,kc->ko", w_real, f_real) - contract("koc,kc->ko", w_imag, f_imag)
    mixed_imag = contract("koc,kc->ko", w_real, f_imag) + contract("koc,kc->ko", w_imag, f_real)
    grad_real = contract("koc,ko->kc", w_real, g_real) + contract("koc,ko->kc", w_imag, g_imag)
    grad_imag = contract("koc,ko->kc", w_real, g_imag) - contract("koc,ko->kc", w_imag, g_real)
    back = jnp.stack([jnp.stack([mixed_real, mixed_imag]), jnp.stack([grad_real, grad_imag])])
    back = back.astype(jnp.bfloat16).reshape(2, 2, MZ, n_blk, chans).transpose(3, 0, 4, 2, 1)
    back = back.reshape(n_blk, 1, 2 * chans * MZ * 2)
    back = lax.all_to_all(back, "blk", 0, 0, tiled=True)
    wide = jnp.float32
    fr, fi, gr, gi = (v.astype(wide) for v in (f_real, f_imag, g_real, g_imag))
    go, fc = (lambda v: v[:, :, None]), (lambda v: v[:, None, :])
    weight_grad = jnp.stack([go(gr) * fc(fr) + go(gi) * fc(fi), go(gi) * fc(fr) - go(gr) * fc(fi)], 1)[None, None]
    back = back.reshape(MY, 2, chans, MZ, 2)
    positions = jnp.arange(NZ, dtype=jnp.int32)
    tables = jnp.stack([z_synthesis_table(positions, amplitude), z_synthesis_table(positions, unit_weights)])
    tables = tables.reshape(2, MZ, 2, n_space, cells, 2)
    scales = jnp.array([synth_scale, forward_scale], jnp.float32)
    zback = jnp.einsum("qhcki,hkiszo->sqhczo", back, tables, preferred_element_type=jnp.float32)
    zback = (zback * scales[None, None, :, None, None, None]).astype(jnp.bfloat16)
    zback = zback.reshape(n_space, MY, 2 * chans * cells * 2)
    zback = lax.all_to_all(zback, "space", 0, 0, tiled=True)
    zback = zback.reshape(MX, MY, 2, chans, cells, 2)
    y_back_table = y_synthesis_table()
    x_back_table = x_synthesis_table()

    def synthesize(h):
        yback = contract("pqczi,iqoy->czopy", zback[:, :, h], y_back_table).astype(jnp.bfloat16)
        return contract("czipy,ipx->czxy", yback, x_back_table).astype(jnp.bfloat16)

    return (synthesize(0), synthesize(1), weight_grad)


def solution(mesh):
    placed = (
        P("blk", "space", None, None),
        P("blk", "space", None, None),
        P("space", "blk", None, None, None, None),
    )
    return jax.shard_map(
        shards,
        mesh=mesh,
        in_specs=placed,
        out_specs=(
            P("blk", "space", None, None),
            P("blk", "space", None, None),
            P("space", "blk", None, None, None, None),
        ),
        check_vma=False,
    )
```

```python
import math

import jax
import jax.numpy as jnp
import numpy as np
from jax import lax
from jax.experimental import pallas as pl
from jax.experimental.pallas import tpu as pltpu
from jax.sharding import PartitionSpec as P

NX = 96
NY = 192
NZ = 96
MX = 16
MY = 32
MZ = 8
CHANS = 4
CELLS = 6
N_SPACE = 16
N_BLK = 32
PAIR = 2
N_LINE = N_BLK // PAIR
QS = MY // PAIR
ROWS = 16
USED = CHANS // 2 * CELLS
LANES = 128
HALF = LANES // 2
MODES = PAIR * 2 * MZ
FORWARD = 1.0 / math.sqrt(NX * NY * NZ)
SYNTH = 1.0 / math.sqrt(MX * MY * MZ)
VMEM_LIMIT = 48 * 1024 * 1024
ALL_VMEM = 63 * 1024 * 1024
F32 = jnp.float32
BF16 = jnp.bfloat16


def freqs(count):
    index = np.arange(count)
    return np.where(index < count // 2, index, index - count)


def phases(frequencies, length):
    product = (frequencies[:, None] * np.arange(length)[None, :]) % length
    angles = product.astype(np.float32) * np.float32(2.0 * math.pi / length)
    return np.cos(angles).astype(np.float32), np.sin(angles).astype(np.float32)


def bf16(table):
    return jnp.asarray(table.astype(BF16))


def y_analysis():
    cosines, sines = (v.T.reshape(NY, PAIR, QS) for v in phases(freqs(MY), NY))
    table = np.zeros((2, NY, 2, PAIR, 2, 2, QS), np.float32)
    for h in range(2):
        table[h, :, 0, :, h, 0] = cosines
        table[h, :, 0, :, h, 1] = -sines
        table[h, :, 1, :, h, 0] = -sines
        table[h, :, 1, :, h, 1] = -cosines
    return bf16(table.reshape(2, NY, 2 * LANES))


def x_analysis():
    cosines, sines = phases(freqs(MX), NX)
    return bf16(np.concatenate([cosines, sines], 0))


def z_table():
    cosines, sines = (v.reshape(MZ, N_SPACE, CELLS) for v in phases(np.arange(MZ), NZ))
    table = np.zeros((2, PAIR, 2, MZ, PAIR, N_SPACE, ROWS), np.float32)
    for pair in range(PAIR):
        for cl in range(2):
            cells = slice(cl * CELLS, (cl + 1) * CELLS)
            table[0, pair, cl, :, pair, :, cells] = cosines
            table[1, pair, cl, :, pair, :, cells] = sines
    return table.reshape(2 * MODES, PAIR * N_SPACE * ROWS)


def x_synthesis():
    cosines, sines = phases(freqs(MX), NX)
    return bf16(np.concatenate([cosines.T, sines.T], 1))


def y_synthesis():
    cosines, sines = (v.reshape(PAIR, QS, NY) for v in phases(freqs(MY), NY))
    table = np.zeros((2, PAIR, 2, 2, QS, NY), np.float32)
    for h in range(2):
        table[h, :, h, 0] = cosines
        table[h, :, h, 1] = -sines
    return bf16(table.reshape(2, LANES, NY))


def dot(a, b):
    return jnp.dot(a, b, preferred_element_type=F32)


def dot_first(a, b):
    return lax.dot_general(a, b, (((0,), (0,)), ((), ())), preferred_element_type=F32)


def dot_last(a, b):
    return lax.dot_general(a, b, (((1,), (1,)), ((), ())), preferred_element_type=F32)


def index(shape, dim):
    return lax.broadcasted_iota(jnp.int32, shape, dim)


def times_minus_i(a):
    real = index(a.shape, 1) // QS % 2 == 0
    return jnp.where(real, pltpu.roll(a, LANES - QS, 1), -pltpu.roll(a, QS, 1))


def times_i(a):
    real = index(a.shape, 1) // QS % 2 == 0
    return jnp.where(real, -pltpu.roll(a, LANES - QS, 1), pltpu.roll(a, QS, 1))


def low_halves(a, b):
    return jnp.where(index(a.shape, 1) < HALF, a, pltpu.roll(b, HALF, 1))


def high_halves(a, b):
    return jnp.where(index(a.shape, 1) < HALF, pltpu.roll(a, HALF, 1), b)


def analyse_kernel(f_hbm, g_hbm, y_hbm, x_hbm, out_ref, f_ref, g_ref, y_ref, x_ref, planes, sems):
    copies = [
        pltpu.make_async_copy(y_hbm, y_ref, sems.at[0]),
        pltpu.make_async_copy(x_hbm, x_ref, sems.at[1]),
    ]
    for c in range(CHANS):
        copies.append(pltpu.make_async_copy(f_hbm.at[c], f_ref.at[c], sems.at[2 + 2 * c]))
        copies.append(pltpu.make_async_copy(g_hbm.at[c], g_ref.at[c], sems.at[3 + 2 * c]))
    for copy in copies:
        copy.start()
    for ch in range(2):
        start = (ch * ROWS + USED) * MX
        planes[start : start + (ROWS - USED) * MX, :] = jnp.zeros(((ROWS - USED) * MX, LANES), F32)
    rows = CELLS * NX
    copies[0].wait()
    copies[1].wait()
    for c in range(CHANS):
        copies[2 + 2 * c].wait()
        copies[3 + 2 * c].wait()
        both = dot(f_ref[c].reshape(rows, NY), y_ref[0]) + dot(g_ref[c].reshape(rows, NY), y_ref[1])
        both = both.astype(BF16)
        for z in range(CELLS):
            part = dot(x_ref[...], both[z * NX : (z + 1) * NX])
            start = (c // 2 * ROWS + c % 2 * CELLS + z) * MX
            planes[start : start + MX, :] = part[:MX, :LANES] + part[MX:, LANES:]
    for p in range(MX):
        first = planes[pl.ds(p, ROWS, stride=MX), :]
        second = planes[pl.ds(ROWS * MX + p, ROWS, stride=MX), :]
        out_ref[p] = low_halves(first, second).astype(BF16)
        out_ref[N_SPACE + p] = high_halves(first, second).astype(BF16)


def message():
    return jax.ShapeDtypeStruct((PAIR * N_SPACE, ROWS, LANES), BF16)


def field_buffer():
    return pltpu.VMEM((CHANS, CELLS, NX, NY), BF16)


def call(kernel, name, out_shape, *operands, in_specs=None, out_specs=None, scratch=(), vmem=VMEM_LIMIT):
    whole = pl.BlockSpec(memory_space=pltpu.VMEM)
    return pl.pallas_call(
        kernel,
        in_specs=in_specs or [whole] * len(operands),
        out_specs=out_specs or jax.tree.map(lambda _: whole, out_shape),
        out_shape=out_shape,
        scratch_shapes=list(scratch),
        compiler_params=pltpu.CompilerParams(vmem_limit_bytes=vmem),
        name=name,
    )(*operands)


def analyse(field, cotangent):
    return call(
        analyse_kernel,
        "analyse",
        message(),
        field,
        cotangent,
        y_analysis(),
        x_analysis(),
        in_specs=[pl.BlockSpec(memory_space=pltpu.HBM)] * 4,
        scratch=[
            field_buffer(),
            field_buffer(),
            pltpu.VMEM((2, NY, 2 * LANES), BF16),
            pltpu.VMEM((2 * MX, NX), BF16),
            pltpu.VMEM((2 * ROWS * MX, LANES), F32),
            pltpu.SemaphoreType.DMA((2 + 2 * CHANS,)),
        ],
        vmem=ALL_VMEM,
    )


def mode_picker(ch):
    shape = (2 * QS, LANES)
    row, lane = index(shape, 0), index(shape, 1)
    return jnp.where(row == lane % QS * 2 + ch, 1.0, 0.0).astype(BF16)


def channel_picker():
    shape = (2 * N_LINE, LANES)
    row, lane = index(shape, 0), index(shape, 1)
    return jnp.where(row == lane // 4 % N_LINE * 2 + lane // 2 % 2, 1.0, 0.0).astype(BF16)


def channel_part(shape):
    lane = index(shape, len(shape) - 1)
    return lane // HALF * 2 + lane % 2


def sum_z_kernel(planes_ref, z_ref, out_ref):
    planes = planes_ref[...].reshape(PAIR * N_SPACE * ROWS, LANES)
    sums = dot(z_ref[...], planes)
    spec = sums[:MODES] + times_minus_i(sums[MODES:])
    field = index(spec.shape, 1) // (2 * QS) % 2
    zero = index(spec.shape, 0) % MZ == 0
    scale = jnp.where(field == 0, FORWARD, jnp.where(zero, SYNTH, 2.0 * SYNTH))
    spec = (spec * scale.astype(F32)).astype(BF16).astype(F32)
    shape = (8, MODES, LANES)
    spread = jnp.where(index(shape, 2) // QS == index(shape, 0), spec[None], 0.0).astype(BF16)
    spread = spread.reshape(8 * MODES, LANES)
    first, second = spread[:LANES], spread[LANES:]
    out_ref[...] = dot_last(mode_picker(0), first) + dot_last(mode_picker(1), second)


def mix_kernel(spec_ref, w_ref, back_ref, chan_ref):
    pick = channel_picker()
    wide = dot_first(spec_ref[...].astype(BF16), pick).reshape(4, 4, MZ, LANES)
    part = channel_part((4, MZ, LANES))
    spec = wide[:, 0]
    for j in range(1, 4):
        spec = jnp.where(part == j, wide[:, j], spec)
    chan_ref[...] = spec.reshape(4 * MZ, LANES)
    fr, fi, gr, gi = (spec[i] for i in range(4))
    f = jnp.concatenate([fr, fi], 0).astype(BF16)
    f_turned = jnp.concatenate([-fi, fr], 0).astype(BF16)
    g = jnp.concatenate([gr, gi], 0).astype(BF16)
    g_turned = jnp.concatenate([gi, -gr], 0).astype(BF16)
    own = index((2 * MZ, LANES), 0) % MZ
    mixed = jnp.zeros((2 * MZ, LANES), F32)
    grad = jnp.zeros((2 * MZ, LANES), F32)
    for k in range(MZ):
        w_real = w_ref[0, 0, k, 0]
        w_imag = w_ref[0, 0, k, 1]
        mixed = jnp.where(own == k, dot_last(f, w_real) + dot_last(f_turned, w_imag), mixed)
        grad = jnp.where(own == k, dot(g, w_real) + dot(g_turned, w_imag), grad)
    back = jnp.concatenate([mixed, grad], 0).reshape(4, 1, MZ, LANES)
    shape = (4, 4, MZ, LANES)
    spread = jnp.where(channel_part(shape) == index(shape, 1), back, 0.0).astype(BF16)
    back_ref[...] = dot_last(pick, spread.reshape(LANES, LANES))


def spread_z_kernel(back_ref, z_ref, out_ref):
    back = back_ref[...].astype(BF16)
    owner = index((MODES, LANES), 1) // QS
    spec = jnp.zeros((MODES, LANES), F32)
    for ch in range(2):
        wide = dot_first(back, mode_picker(ch)).reshape(4, MODES, LANES)
        for part in range(4):
            spec = jnp.where(owner == 4 * ch + part, wide[part], spec)
    field = owner // 2 % 2
    zero = index(spec.shape, 0) % MZ == 0
    spec = jnp.where((field == 0) & ~zero, 2.0 * spec, spec)
    stacked = jnp.concatenate([spec, times_i(spec)], 0).astype(BF16)
    lane = index((1, LANES), 1) // (2 * QS) % 2
    scale = jnp.where(lane == 0, SYNTH, FORWARD).astype(F32)
    zback = (dot(z_ref[...], stacked) * scale).astype(BF16)
    out_ref[...] = zback.reshape(PAIR * N_SPACE, ROWS, LANES)


def synthesize_kernel(zback_ref, x_ref, y_ref, out_hbm, grad_hbm, out_ref, grad_ref, planes, sems):
    planes[...] = zback_ref[...].astype(F32).reshape(PAIR * N_SPACE * ROWS, LANES)
    copies = []
    for c in range(CHANS):
        parts = []
        for z in range(CELLS):
            row = c % 2 * CELLS + z
            first = planes[pl.ds(row, MX, stride=ROWS), :]
            second = planes[pl.ds(MX * ROWS + row, MX, stride=ROWS), :]
            plane = low_halves(first, second) if c < 2 else high_halves(first, second)
            stacked = jnp.concatenate([plane, times_i(plane)], 0).astype(BF16)
            parts.append(dot(x_ref[...], stacked).astype(BF16))
        both = jnp.concatenate(parts, 0)
        for i, (buffer, target) in enumerate(((out_ref, out_hbm), (grad_ref, grad_hbm))):
            buffer[c] = dot(both, y_ref[i]).astype(BF16).reshape(CELLS, NX, NY)
            copy = pltpu.make_async_copy(buffer.at[c], target.at[c], sems.at[2 * c + i])
            copy.start()
            copies.append(copy)
    for copy in copies:
        copy.wait()


def synthesize(zback):
    shape = jax.ShapeDtypeStruct((CHANS, CELLS, NX, NY), BF16)
    return call(
        synthesize_kernel,
        "synthesize",
        (shape, shape),
        zback,
        x_synthesis(),
        y_synthesis(),
        out_specs=(pl.BlockSpec(memory_space=pltpu.HBM),) * 2,
        scratch=[
            field_buffer(),
            field_buffer(),
            pltpu.VMEM((PAIR * N_SPACE * ROWS, LANES), F32),
            pltpu.SemaphoreType.DMA((2 * CHANS,)),
        ],
    )


def outer(values):
    groups = [
        [(pair * N_LINE + line) * N_SPACE + s for pair in range(PAIR) for s in range(N_SPACE)]
        for line in range(N_LINE)
    ]
    return lax.all_to_all(values, ("blk", "space"), 0, 0, tiled=True, axis_index_groups=groups)


def inner(values):
    groups = [[pair * N_LINE + line for line in range(N_LINE)] for pair in range(PAIR)]
    values = values.reshape(N_LINE, 2, LANES)
    values = lax.all_to_all(values, "blk", 0, 0, tiled=True, axis_index_groups=groups)
    return values.reshape(2 * N_LINE, LANES)


def shards(input_field, cotangent, weights):
    planes = outer(analyse(input_field, cotangent))
    small = jax.ShapeDtypeStruct((2 * N_LINE, LANES), F32)
    table = z_table()
    spec = inner(call(sum_z_kernel, "sum_z", small, planes, bf16(table)))
    back, chan = call(mix_kernel, "mix", (small, small), spec, weights)
    back = inner(back)
    fr, fi, gr, gi = (chan[i * MZ : (i + 1) * MZ] for i in range(4))
    go, fc = (lambda v: v[:, :, None]), (lambda v: v[:, None, :])
    weight_grad = jnp.stack([go(gr) * fc(fr) + go(gi) * fc(fi), go(gi) * fc(fr) - go(gr) * fc(fi)], 1)[None, None]
    zback = outer(call(spread_z_kernel, "spread_z", message(), back, bf16(table.T)))
    spectral_out, field_grad = synthesize(zback)
    return (spectral_out, field_grad, weight_grad)


def solution(mesh):
    fields = P("blk", "space", None, None)
    modes = P("space", "blk", None, None, None, None)
    return jax.shard_map(
        shards,
        mesh=mesh,
        in_specs=(fields, fields, modes),
        out_specs=(fields, fields, modes),
        check_vma=False,
    )
```

```python
import math

import jax
import jax.numpy as jnp
import numpy as np
from jax import lax
from jax.experimental import pallas as pl
from jax.experimental.pallas import tpu as pltpu
from jax.sharding import PartitionSpec as P

NX = 96
NY = 192
NZ = 96
MX = 16
MY = 32
MZ = 8
CHANS = 4
CELLS = 6
N_SPACE = 16
N_BLK = 32
PAIR = 2
N_LINE = N_BLK // PAIR
QS = MY // PAIR
ROWS = 16
USED = CHANS // 2 * CELLS
LANES = 128
HALF = LANES // 2
MODES = PAIR * 2 * MZ
FORWARD = 1.0 / math.sqrt(NX * NY * NZ)
SYNTH = 1.0 / math.sqrt(MX * MY * MZ)
VMEM_LIMIT = 48 * 1024 * 1024
F32 = jnp.float32
BF16 = jnp.bfloat16


def freqs(count):
    index = np.arange(count)
    return np.where(index < count // 2, index, index - count)


def phases(frequencies, length):
    product = (frequencies[:, None] * np.arange(length)[None, :]) % length
    angles = product.astype(np.float32) * np.float32(2.0 * math.pi / length)
    return np.cos(angles).astype(np.float32), np.sin(angles).astype(np.float32)


def bf16(table):
    return jnp.asarray(table.astype(BF16))


def y_analysis():
    cosines, sines = (v.T.reshape(NY, PAIR, QS) for v in phases(freqs(MY), NY))
    table = np.zeros((2, 2, NY, PAIR, 2, 2, QS), np.float32)
    for h in range(2):
        table[h, 0, :, :, h, 0] = cosines
        table[h, 0, :, :, h, 1] = -sines
        table[h, 1, :, :, h, 0] = -sines
        table[h, 1, :, :, h, 1] = -cosines
    return bf16(table.reshape(2, 2, NY, LANES))


def x_analysis():
    cosines, sines = phases(freqs(MX), NX)
    return bf16(np.concatenate([cosines, sines], 0))


def z_table():
    cosines, sines = (v.reshape(MZ, N_SPACE, CELLS) for v in phases(np.arange(MZ), NZ))
    table = np.zeros((2, PAIR, 2, MZ, PAIR, N_SPACE, ROWS), np.float32)
    for pair in range(PAIR):
        for cl in range(2):
            cells = slice(cl * CELLS, (cl + 1) * CELLS)
            table[0, pair, cl, :, pair, :, cells] = cosines
            table[1, pair, cl, :, pair, :, cells] = sines
    return table.reshape(2 * MODES, PAIR * N_SPACE * ROWS)


def x_synthesis():
    cosines, sines = phases(freqs(MX), NX)
    return bf16(np.concatenate([cosines.T, sines.T], 1))


def y_synthesis():
    cosines, sines = (v.reshape(PAIR, QS, NY) for v in phases(freqs(MY), NY))
    table = np.zeros((2, PAIR, 2, 2, QS, NY), np.float32)
    for h in range(2):
        table[h, :, h, 0] = cosines
        table[h, :, h, 1] = -sines
    return bf16(table.reshape(2, LANES, NY))


def dot(a, b):
    return jnp.dot(a, b, preferred_element_type=F32)


def dot_first(a, b):
    return lax.dot_general(a, b, (((0,), (0,)), ((), ())), preferred_element_type=F32)


def dot_last(a, b):
    return lax.dot_general(a, b, (((1,), (1,)), ((), ())), preferred_element_type=F32)


def index(shape, dim):
    return lax.broadcasted_iota(jnp.int32, shape, dim)


def times_minus_i(a):
    real = index(a.shape, 1) // QS % 2 == 0
    return jnp.where(real, pltpu.roll(a, LANES - QS, 1), -pltpu.roll(a, QS, 1))


def times_i(a):
    real = index(a.shape, 1) // QS % 2 == 0
    return jnp.where(real, -pltpu.roll(a, LANES - QS, 1), pltpu.roll(a, QS, 1))


def low_halves(a, b):
    return jnp.where(index(a.shape, 1) < HALF, a, pltpu.roll(b, HALF, 1))


def high_halves(a, b):
    return jnp.where(index(a.shape, 1) < HALF, pltpu.roll(a, HALF, 1), b)


def analyse_kernel(f_hbm, g_hbm, y_hbm, x_hbm, out_ref, f_ref, g_ref, y_ref, x_ref, sums, planes, sems):
    copies = [
        pltpu.make_async_copy(y_hbm, y_ref, sems.at[0]),
        pltpu.make_async_copy(x_hbm, x_ref, sems.at[1]),
    ]
    for c in range(CHANS):
        copies.append(pltpu.make_async_copy(f_hbm.at[c], f_ref.at[c], sems.at[2 + 2 * c]))
        copies.append(pltpu.make_async_copy(g_hbm.at[c], g_ref.at[c], sems.at[3 + 2 * c]))
    for copy in copies:
        copy.start()
    for ch in range(2):
        start = (ch * ROWS + USED) * MX
        planes[start : start + (ROWS - USED) * MX, :] = jnp.zeros(((ROWS - USED) * MX, LANES), F32)
    rows = CELLS * NX
    copies[0].wait()
    copies[1].wait()
    for c in range(CHANS):
        copies[2 + 2 * c].wait()
        copies[3 + 2 * c].wait()
        for h, v in enumerate((f_ref, g_ref)):
            for z in range(CELLS):
                part = dot(x_ref[...], v[c, z]).astype(BF16)
                start = (c * CELLS + z) * MX
                for r in range(2):
                    sums[h, r, start : start + MX, :] = part[r * MX : (r + 1) * MX]
    total = 0.0
    for h in range(2):
        for r in range(2):
            total = total + dot(sums[h, r], y_ref[h, r])
    for ch in range(2):
        start = ch * ROWS * MX
        planes[start : start + USED * MX, :] = total[ch * USED * MX : (ch + 1) * USED * MX]
    for p in range(MX):
        first = planes[pl.ds(p, ROWS, stride=MX), :]
        second = planes[pl.ds(ROWS * MX + p, ROWS, stride=MX), :]
        out_ref[p] = low_halves(first, second).astype(BF16)
        out_ref[N_SPACE + p] = high_halves(first, second).astype(BF16)


def in_hbm(values):
    return pltpu.with_memory_space_constraint(values, pltpu.HBM)


def message():
    return jax.ShapeDtypeStruct((PAIR * N_SPACE, ROWS, LANES), BF16)


def small_message():
    return jax.ShapeDtypeStruct((2 * N_LINE, LANES), F32)


def field_buffer():
    return pltpu.VMEM((CHANS, CELLS, NX, NY), BF16)


def call(kernel, name, out_shape, *operands, in_specs=None, out_specs=None, scratch=()):
    whole = pl.BlockSpec(memory_space=pltpu.VMEM)
    return pl.pallas_call(
        kernel,
        in_specs=in_specs or [whole] * len(operands),
        out_specs=out_specs or jax.tree.map(lambda _: whole, out_shape),
        out_shape=out_shape,
        scratch_shapes=list(scratch),
        compiler_params=pltpu.CompilerParams(vmem_limit_bytes=VMEM_LIMIT),
        name=name,
    )(*operands)


def analyse(field, cotangent):
    return call(
        analyse_kernel,
        "analyse",
        message(),
        *(in_hbm(v) for v in (field, cotangent, y_analysis(), x_analysis())),
        in_specs=[pl.BlockSpec(memory_space=pltpu.HBM)] * 4,
        scratch=[
            field_buffer(),
            field_buffer(),
            pltpu.VMEM((2, 2, NY, LANES), BF16),
            pltpu.VMEM((2 * MX, NX), BF16),
            pltpu.VMEM((2, 2, 4 * CELLS * MX, NY), BF16),
            pltpu.VMEM((2 * ROWS * MX, LANES), F32),
            pltpu.SemaphoreType.DMA((2 + 2 * CHANS,)),
        ],
    )


def mode_picker(ch):
    shape = (2 * QS, LANES)
    row, lane = index(shape, 0), index(shape, 1)
    return jnp.where(row == lane % QS * 2 + ch, 1.0, 0.0).astype(BF16)


def channel_picker():
    shape = (2 * N_LINE, LANES)
    row, lane = index(shape, 0), index(shape, 1)
    return jnp.where(row == lane // 4 % N_LINE * 2 + lane // 2 % 2, 1.0, 0.0).astype(BF16)


def channel_part(shape):
    lane = index(shape, len(shape) - 1)
    return lane // HALF * 2 + lane % 2


def sum_z_kernel(planes_ref, z_ref, out_ref):
    planes = planes_ref[...].reshape(PAIR * N_SPACE * ROWS, LANES)
    sums = dot(z_ref[...], planes)
    spec = sums[:MODES] + times_minus_i(sums[MODES:])
    field = index(spec.shape, 1) // (2 * QS) % 2
    zero = index(spec.shape, 0) % MZ == 0
    scale = jnp.where(field == 0, FORWARD, jnp.where(zero, SYNTH, 2.0 * SYNTH))
    spec = (spec * scale.astype(F32)).astype(BF16).astype(F32)
    shape = (8, MODES, LANES)
    spread = jnp.where(index(shape, 2) // QS == index(shape, 0), spec[None], 0.0).astype(BF16)
    spread = spread.reshape(8 * MODES, LANES)
    first, second = spread[:LANES], spread[LANES:]
    out_ref[...] = dot_last(mode_picker(0), first) + dot_last(mode_picker(1), second)


def mix_kernel(spec_ref, w_ref, back_ref, chan_ref):
    pick = channel_picker()
    wide = dot_first(spec_ref[...].astype(BF16), pick).reshape(4, 4, MZ, LANES)
    part = channel_part((4, MZ, LANES))
    spec = wide[:, 0]
    for j in range(1, 4):
        spec = jnp.where(part == j, wide[:, j], spec)
    chan_ref[...] = spec.reshape(4 * MZ, LANES)
    fr, fi, gr, gi = (spec[i] for i in range(4))
    f = jnp.concatenate([fr, fi], 0).astype(BF16)
    g = jnp.concatenate([gr, gi], 0).astype(BF16)
    own = index((2 * MZ, 2 * LANES), 0) % MZ
    by_f = jnp.zeros((2 * MZ, 2 * LANES), F32)
    by_g = jnp.zeros((2 * MZ, 2 * LANES), F32)
    for k in range(MZ):
        both = w_ref[0, 0, k]
        by_f = jnp.where(own == k, dot_last(f, both.reshape(2 * LANES, LANES)), by_f)
        by_g = jnp.where(own == k, dot(g, jnp.concatenate([both[0], both[1]], 1)), by_g)
    mixed_real = by_f[:MZ, :LANES] - by_f[MZ:, LANES:]
    mixed_imag = by_f[MZ:, :LANES] + by_f[:MZ, LANES:]
    grad_real = by_g[:MZ, :LANES] + by_g[MZ:, LANES:]
    grad_imag = by_g[MZ:, :LANES] - by_g[:MZ, LANES:]
    back = jnp.concatenate([mixed_real, mixed_imag, grad_real, grad_imag], 0)
    back = back.reshape(4, 1, MZ, LANES)
    shape = (4, 4, MZ, LANES)
    spread = jnp.where(channel_part(shape) == index(shape, 1), back, 0.0).astype(BF16)
    back_ref[...] = dot_last(pick, spread.reshape(LANES, LANES))


def spread_z_kernel(back_ref, z_ref, out_ref):
    back = back_ref[...].astype(BF16)
    owner = index((MODES, LANES), 1) // QS
    spec = jnp.zeros((MODES, LANES), F32)
    for ch in range(2):
        wide = dot_first(back, mode_picker(ch)).reshape(4, MODES, LANES)
        for part in range(4):
            spec = jnp.where(owner == 4 * ch + part, wide[part], spec)
    field = owner // 2 % 2
    zero = index(spec.shape, 0) % MZ == 0
    spec = jnp.where((field == 0) & ~zero, 2.0 * spec, spec)
    stacked = jnp.concatenate([spec, times_i(spec)], 0).astype(BF16)
    lane = index((1, LANES), 1) // (2 * QS) % 2
    scale = jnp.where(lane == 0, SYNTH, FORWARD).astype(F32)
    zback = (dot(z_ref[...], stacked) * scale).astype(BF16)
    out_ref[...] = zback.reshape(PAIR * N_SPACE, ROWS, LANES)


def synthesize_kernel(
    zback_ref, chan_ref, x_ref, y_ref, out_hbm, grad_hbm, wgrad_hbm, out_ref, grad_ref, wgrad_ref, planes, mids, sems
):
    copies = []

    def send(source, target):
        copy = pltpu.make_async_copy(source, target, sems.at[len(copies)])
        copy.start()
        copies.append(copy)

    planes[...] = zback_ref[...].astype(F32).reshape(PAIR * N_SPACE * ROWS, LANES)
    columns = chan_ref[2 * MZ :, :].T
    for k in range(MZ):
        fr, fi = (chan_ref[i * MZ + k : i * MZ + k + 1, :] for i in range(2))
        gr, gi = (columns[:, i * MZ + k : i * MZ + k + 1] for i in range(2))
        wgrad_ref[k, 0] = gr * fr + gi * fi
        wgrad_ref[k, 1] = gi * fr - gr * fi
    send(wgrad_ref, wgrad_hbm.at[0, 0])
    for c in range(CHANS):
        for z in range(CELLS):
            row = c % 2 * CELLS + z
            first = planes[pl.ds(row, MX, stride=ROWS), :]
            second = planes[pl.ds(MX * ROWS + row, MX, stride=ROWS), :]
            plane = low_halves(first, second) if c < 2 else high_halves(first, second)
            stacked = jnp.concatenate([plane, times_i(plane)], 0).astype(BF16)
            mids[c, z * NX : (z + 1) * NX, :] = dot(x_ref[...], stacked).astype(BF16)
    for c in range(CHANS):
        both = mids[c]
        for i, (buffer, target) in enumerate(((out_ref, out_hbm), (grad_ref, grad_hbm))):
            buffer[c] = dot(both, y_ref[i]).astype(BF16).reshape(CELLS, NX, NY)
            send(buffer.at[c], target.at[c])
    for copy in copies:
        copy.wait()


def synthesize(zback, chan):
    shape = jax.ShapeDtypeStruct((CHANS, CELLS, NX, NY), BF16)
    wgrad = (MZ, 2, LANES, LANES)
    return call(
        synthesize_kernel,
        "synthesize",
        (shape, shape, jax.ShapeDtypeStruct((1, 1) + wgrad, F32)),
        zback,
        chan,
        x_synthesis(),
        y_synthesis(),
        out_specs=(pl.BlockSpec(memory_space=pltpu.HBM),) * 3,
        scratch=[
            field_buffer(),
            field_buffer(),
            pltpu.VMEM(wgrad, F32),
            pltpu.VMEM((PAIR * N_SPACE * ROWS, LANES), F32),
            pltpu.VMEM((CHANS, CELLS * NX, LANES), BF16),
            pltpu.SemaphoreType.DMA((2 * CHANS + 1,)),
        ],
    )


def outer(values):
    groups = [
        [(pair * N_LINE + line) * N_SPACE + s for pair in range(PAIR) for s in range(N_SPACE)]
        for line in range(N_LINE)
    ]
    return lax.all_to_all(values, ("blk", "space"), 0, 0, tiled=True, axis_index_groups=groups)


def inner(values):
    groups = [[pair * N_LINE + line for line in range(N_LINE)] for pair in range(PAIR)]
    values = values.reshape(N_LINE, 2, LANES)
    values = lax.all_to_all(values, "blk", 0, 0, tiled=True, axis_index_groups=groups)
    return values.reshape(2 * N_LINE, LANES)


def sum_z(planes):
    return call(sum_z_kernel, "sum_z", small_message(), planes, bf16(z_table()))


def mix(spec, weights):
    return call(mix_kernel, "mix", (small_message(), small_message()), spec, weights)


def spread_z(back):
    return call(spread_z_kernel, "spread_z", message(), back, bf16(z_table().T))


def shards(input_field, cotangent, weights):
    planes = outer(analyse(input_field, cotangent))
    spec = inner(sum_z(planes))
    back, chan = mix(spec, weights)
    back = inner(back)
    zback = outer(spread_z(back))
    return synthesize(zback, chan)


def solution(mesh):
    fields = P("blk", "space", None, None)
    modes = P("space", "blk", None, None, None, None)
    return jax.shard_map(
        shards,
        mesh=mesh,
        in_specs=(fields, fields, modes),
        out_specs=(fields, fields, modes),
        check_vma=False,
    )
```

```python
import math

import jax
import jax.numpy as jnp
import numpy as np
from jax import lax
from jax.experimental import pallas as pl
from jax.experimental.pallas import tpu as pltpu
from jax.sharding import PartitionSpec as P

NX = 96
NY = 192
NZ = 96
MX = 16
MY = 32
MZ = 8
CHANS = 4
CELLS = 6
N_SPACE = 16
N_BLK = 32
PAIR = 2
N_LINE = N_BLK // PAIR
QS = MY // PAIR
ROWS = 16
USED = CHANS // 2 * CELLS
LANES = 128
HALF = LANES // 2
MODES = PAIR * 2 * MZ
FORWARD = 1.0 / math.sqrt(NX * NY * NZ)
SYNTH = 1.0 / math.sqrt(MX * MY * MZ)
VMEM_LIMIT = 48 * 1024 * 1024
LEAD_X = 2
LEAD_Z = 5
LEAD_LINE = 9
F32 = jnp.float32
BF16 = jnp.bfloat16


OUTER = [
    ((LEAD_Z + z) % 8 % 2, (LEAD_X + x) % 4 * 4 + (LEAD_Z + z) % 8 // 2) for x in range(4) for z in range(8)
]
PLACE = {member: place for place, member in enumerate(OUTER)}


def freqs(count):
    index = np.arange(count)
    return np.where(index < count // 2, index, index - count)


def phases(frequencies, length):
    product = (frequencies[:, None] * np.arange(length)[None, :]) % length
    angles = product.astype(np.float32) * np.float32(2.0 * math.pi / length)
    return np.cos(angles).astype(np.float32), np.sin(angles).astype(np.float32)


def bf16(table):
    return jnp.asarray(table.astype(BF16))


def y_analysis():
    cosines, sines = (v.T.reshape(NY, PAIR, QS) for v in phases(freqs(MY), NY))
    table = np.zeros((2, 2, NY, PAIR, 2, 2, QS), np.float32)
    for h in range(2):
        table[h, 0, :, :, h, 0] = cosines
        table[h, 0, :, :, h, 1] = -sines
        table[h, 1, :, :, h, 0] = -sines
        table[h, 1, :, :, h, 1] = -cosines
    return bf16(table.reshape(2, 2, NY, LANES))


def x_analysis():
    cosines, sines = phases(freqs(MX), NX)
    return bf16(np.concatenate([cosines, sines], 0))


def z_table():
    cosines, sines = (v.reshape(MZ, N_SPACE, CELLS) for v in phases(np.arange(MZ), NZ))
    table = np.zeros((2, PAIR, 2, MZ, PAIR, N_SPACE, ROWS), np.float32)
    for pair in range(PAIR):
        for cl in range(2):
            cells = slice(cl * CELLS, (cl + 1) * CELLS)
            table[0, pair, cl, :, pair, :, cells] = cosines
            table[1, pair, cl, :, pair, :, cells] = sines
    table = table.reshape(2 * MODES, PAIR * N_SPACE, ROWS)[:, [pair * N_SPACE + space for pair, space in OUTER]]
    return table.reshape(2 * MODES, PAIR * N_SPACE * ROWS)


def x_synthesis():
    cosines, sines = phases(freqs(MX), NX)
    return bf16(np.concatenate([cosines.T, sines.T], 1))


def y_synthesis():
    cosines, sines = (v.reshape(PAIR, QS, NY) for v in phases(freqs(MY), NY))
    table = np.zeros((2, PAIR, 2, 2, QS, NY), np.float32)
    for h in range(2):
        table[h, :, h, 0] = cosines
        table[h, :, h, 1] = -sines
    return bf16(table.reshape(2, LANES, NY))


def dot(a, b):
    return jnp.dot(a, b, preferred_element_type=F32)


def dot_first(a, b):
    return lax.dot_general(a, b, (((0,), (0,)), ((), ())), preferred_element_type=F32)


def dot_last(a, b):
    return lax.dot_general(a, b, (((1,), (1,)), ((), ())), preferred_element_type=F32)


def index(shape, dim):
    return lax.broadcasted_iota(jnp.int32, shape, dim)


def times_minus_i(a):
    real = index(a.shape, 1) // QS % 2 == 0
    return jnp.where(real, pltpu.roll(a, LANES - QS, 1), -pltpu.roll(a, QS, 1))


def times_i(a):
    real = index(a.shape, 1) // QS % 2 == 0
    return jnp.where(real, -pltpu.roll(a, LANES - QS, 1), pltpu.roll(a, QS, 1))


def low_halves(a, b):
    return jnp.where(index(a.shape, 1) < HALF, a, pltpu.roll(b, HALF, 1))


def high_halves(a, b):
    return jnp.where(index(a.shape, 1) < HALF, pltpu.roll(a, HALF, 1), b)


def analyse_kernel(f_hbm, g_hbm, y_hbm, x_hbm, out_ref, f_ref, g_ref, y_ref, x_ref, sums, planes, sems):
    copies = [
        pltpu.make_async_copy(y_hbm, y_ref, sems.at[0]),
        pltpu.make_async_copy(x_hbm, x_ref, sems.at[1]),
    ]
    for c in range(CHANS):
        copies.append(pltpu.make_async_copy(f_hbm.at[c], f_ref.at[c], sems.at[2 + 2 * c]))
        copies.append(pltpu.make_async_copy(g_hbm.at[c], g_ref.at[c], sems.at[3 + 2 * c]))
    for copy in copies:
        copy.start()
    for ch in range(2):
        start = (ch * ROWS + USED) * MX
        planes[start : start + (ROWS - USED) * MX, :] = jnp.zeros(((ROWS - USED) * MX, LANES), F32)
    rows = CELLS * NX
    copies[0].wait()
    copies[1].wait()
    for c in range(CHANS):
        copies[2 + 2 * c].wait()
        copies[3 + 2 * c].wait()
        for h, v in enumerate((f_ref, g_ref)):
            for z in range(CELLS):
                part = dot(x_ref[...], v[c, z]).astype(BF16)
                start = (c * CELLS + z) * MX
                for r in range(2):
                    sums[h, r, start : start + MX, :] = part[r * MX : (r + 1) * MX]
    total = 0.0
    for h in range(2):
        for r in range(2):
            total = total + dot(sums[h, r], y_ref[h, r])
    for ch in range(2):
        start = ch * ROWS * MX
        planes[start : start + USED * MX, :] = total[ch * USED * MX : (ch + 1) * USED * MX]
    for p in range(MX):
        first = planes[pl.ds(p, ROWS, stride=MX), :]
        second = planes[pl.ds(ROWS * MX + p, ROWS, stride=MX), :]
        out_ref[PLACE[0, p]] = low_halves(first, second).astype(BF16)
        out_ref[PLACE[1, p]] = high_halves(first, second).astype(BF16)


def in_hbm(values):
    return pltpu.with_memory_space_constraint(values, pltpu.HBM)


def message():
    return jax.ShapeDtypeStruct((PAIR * N_SPACE, ROWS, LANES), BF16)


def small_message():
    return jax.ShapeDtypeStruct((2 * N_LINE, LANES), F32)


def field_buffer():
    return pltpu.VMEM((CHANS, CELLS, NX, NY), BF16)


def call(kernel, name, out_shape, *operands, in_specs=None, out_specs=None, scratch=()):
    whole = pl.BlockSpec(memory_space=pltpu.VMEM)
    return pl.pallas_call(
        kernel,
        in_specs=in_specs or [whole] * len(operands),
        out_specs=out_specs or jax.tree.map(lambda _: whole, out_shape),
        out_shape=out_shape,
        scratch_shapes=list(scratch),
        compiler_params=pltpu.CompilerParams(vmem_limit_bytes=VMEM_LIMIT),
        name=name,
    )(*operands)


def analyse(field, cotangent):
    return call(
        analyse_kernel,
        "analyse",
        message(),
        *(in_hbm(v) for v in (field, cotangent, y_analysis(), x_analysis())),
        in_specs=[pl.BlockSpec(memory_space=pltpu.HBM)] * 4,
        scratch=[
            field_buffer(),
            field_buffer(),
            pltpu.VMEM((2, 2, NY, LANES), BF16),
            pltpu.VMEM((2 * MX, NX), BF16),
            pltpu.VMEM((2, 2, 4 * CELLS * MX, NY), BF16),
            pltpu.VMEM((2 * ROWS * MX, LANES), F32),
            pltpu.SemaphoreType.DMA((2 + 2 * CHANS,)),
        ],
    )


def line_place(line):
    return (line + N_LINE - LEAD_LINE) % N_LINE


def mode_picker(ch):
    shape = (2 * QS, LANES)
    row, lane = index(shape, 0), index(shape, 1)
    return jnp.where(row == line_place(lane % QS) * 2 + ch, 1.0, 0.0).astype(BF16)


def channel_picker():
    shape = (2 * N_LINE, LANES)
    row, lane = index(shape, 0), index(shape, 1)
    return jnp.where(row == line_place(lane // 4 % N_LINE) * 2 + lane // 2 % 2, 1.0, 0.0).astype(BF16)


def channel_part(shape):
    lane = index(shape, len(shape) - 1)
    return lane // HALF * 2 + lane % 2


def sum_z_kernel(planes_ref, z_ref, out_ref):
    planes = planes_ref[...].reshape(PAIR * N_SPACE * ROWS, LANES)
    sums = dot(z_ref[...], planes)
    spec = sums[:MODES] + times_minus_i(sums[MODES:])
    field = index(spec.shape, 1) // (2 * QS) % 2
    zero = index(spec.shape, 0) % MZ == 0
    scale = jnp.where(field == 0, FORWARD, jnp.where(zero, SYNTH, 2.0 * SYNTH))
    spec = (spec * scale.astype(F32)).astype(BF16).astype(F32)
    shape = (8, MODES, LANES)
    spread = jnp.where(index(shape, 2) // QS == index(shape, 0), spec[None], 0.0).astype(BF16)
    spread = spread.reshape(8 * MODES, LANES)
    first, second = spread[:LANES], spread[LANES:]
    out_ref[...] = dot_last(mode_picker(0), first) + dot_last(mode_picker(1), second)


def mix_kernel(spec_ref, w_ref, back_ref, chan_ref):
    pick = channel_picker()
    wide = dot_first(spec_ref[...].astype(BF16), pick).reshape(4, 4, MZ, LANES)
    part = channel_part((4, MZ, LANES))
    spec = wide[:, 0]
    for j in range(1, 4):
        spec = jnp.where(part == j, wide[:, j], spec)
    chan_ref[...] = spec.reshape(4 * MZ, LANES)
    fr, fi, gr, gi = (spec[i] for i in range(4))
    f = jnp.concatenate([fr, fi], 0).astype(BF16)
    g = jnp.concatenate([gr, gi], 0).astype(BF16)
    own = index((2 * MZ, 2 * LANES), 0) % MZ
    by_f = jnp.zeros((2 * MZ, 2 * LANES), F32)
    by_g = jnp.zeros((2 * MZ, 2 * LANES), F32)
    for k in range(MZ):
        both = w_ref[0, 0, k]
        by_f = jnp.where(own == k, dot_last(f, both.reshape(2 * LANES, LANES)), by_f)
        by_g = jnp.where(own == k, dot(g, jnp.concatenate([both[0], both[1]], 1)), by_g)
    mixed_real = by_f[:MZ, :LANES] - by_f[MZ:, LANES:]
    mixed_imag = by_f[MZ:, :LANES] + by_f[:MZ, LANES:]
    grad_real = by_g[:MZ, :LANES] + by_g[MZ:, LANES:]
    grad_imag = by_g[MZ:, :LANES] - by_g[:MZ, LANES:]
    back = jnp.concatenate([mixed_real, mixed_imag, grad_real, grad_imag], 0)
    back = back.reshape(4, 1, MZ, LANES)
    shape = (4, 4, MZ, LANES)
    spread = jnp.where(channel_part(shape) == index(shape, 1), back, 0.0).astype(BF16)
    back_ref[...] = dot_last(pick, spread.reshape(LANES, LANES))


def spread_z_kernel(back_ref, z_ref, out_ref):
    back = back_ref[...].astype(BF16)
    owner = index((MODES, LANES), 1) // QS
    spec = jnp.zeros((MODES, LANES), F32)
    for ch in range(2):
        wide = dot_first(back, mode_picker(ch)).reshape(4, MODES, LANES)
        for part in range(4):
            spec = jnp.where(owner == 4 * ch + part, wide[part], spec)
    field = owner // 2 % 2
    zero = index(spec.shape, 0) % MZ == 0
    spec = jnp.where((field == 0) & ~zero, 2.0 * spec, spec)
    stacked = jnp.concatenate([spec, times_i(spec)], 0).astype(BF16)
    lane = index((1, LANES), 1) // (2 * QS) % 2
    scale = jnp.where(lane == 0, SYNTH, FORWARD).astype(F32)
    zback = (dot(z_ref[...], stacked) * scale).astype(BF16)
    out_ref[...] = zback.reshape(PAIR * N_SPACE, ROWS, LANES)


def synthesize_kernel(
    zback_ref, chan_ref, x_ref, y_ref, out_hbm, grad_hbm, wgrad_hbm, out_ref, grad_ref, wgrad_ref, planes, mids, sems
):
    copies = []

    def send(source, target):
        copy = pltpu.make_async_copy(source, target, sems.at[len(copies)])
        copy.start()
        copies.append(copy)

    for place, (pair, space) in enumerate(OUTER):
        start = (pair * N_SPACE + space) * ROWS
        planes[start : start + ROWS, :] = zback_ref[place].astype(F32)
    columns = chan_ref[2 * MZ :, :].T
    for k in range(MZ):
        fr, fi = (chan_ref[i * MZ + k : i * MZ + k + 1, :] for i in range(2))
        gr, gi = (columns[:, i * MZ + k : i * MZ + k + 1] for i in range(2))
        wgrad_ref[k, 0] = gr * fr + gi * fi
        wgrad_ref[k, 1] = gi * fr - gr * fi
    send(wgrad_ref, wgrad_hbm.at[0, 0])
    for c in range(CHANS):
        for z in range(CELLS):
            row = c % 2 * CELLS + z
            first = planes[pl.ds(row, MX, stride=ROWS), :]
            second = planes[pl.ds(MX * ROWS + row, MX, stride=ROWS), :]
            plane = low_halves(first, second) if c < 2 else high_halves(first, second)
            stacked = jnp.concatenate([plane, times_i(plane)], 0).astype(BF16)
            mids[c, z * NX : (z + 1) * NX, :] = dot(x_ref[...], stacked).astype(BF16)
    for c in range(CHANS):
        both = mids[c]
        for i, (buffer, target) in enumerate(((out_ref, out_hbm), (grad_ref, grad_hbm))):
            buffer[c] = dot(both, y_ref[i]).astype(BF16).reshape(CELLS, NX, NY)
            send(buffer.at[c], target.at[c])
    for copy in copies:
        copy.wait()


def synthesize(zback, chan):
    shape = jax.ShapeDtypeStruct((CHANS, CELLS, NX, NY), BF16)
    wgrad = (MZ, 2, LANES, LANES)
    return call(
        synthesize_kernel,
        "synthesize",
        (shape, shape, jax.ShapeDtypeStruct((1, 1) + wgrad, F32)),
        zback,
        chan,
        x_synthesis(),
        y_synthesis(),
        out_specs=(pl.BlockSpec(memory_space=pltpu.HBM),) * 3,
        scratch=[
            field_buffer(),
            field_buffer(),
            pltpu.VMEM(wgrad, F32),
            pltpu.VMEM((PAIR * N_SPACE * ROWS, LANES), F32),
            pltpu.VMEM((CHANS, CELLS * NX, LANES), BF16),
            pltpu.SemaphoreType.DMA((2 * CHANS + 1,)),
        ],
    )


def outer(values):
    groups = [[(pair * N_LINE + line) * N_SPACE + space for pair, space in OUTER] for line in range(N_LINE)]
    return lax.all_to_all(values, ("blk", "space"), 0, 0, tiled=True, axis_index_groups=groups)


def inner(values):
    lines = [(LEAD_LINE + place) % N_LINE for place in range(N_LINE)]
    groups = [[pair * N_LINE + line for line in lines] for pair in range(PAIR)]
    values = values.reshape(N_LINE, 2, LANES)
    values = lax.all_to_all(values, "blk", 0, 0, tiled=True, axis_index_groups=groups)
    return values.reshape(2 * N_LINE, LANES)


def sum_z(planes):
    return call(sum_z_kernel, "sum_z", small_message(), planes, bf16(z_table()))


def mix(spec, weights):
    return call(mix_kernel, "mix", (small_message(), small_message()), spec, weights)


def spread_z(back):
    return call(spread_z_kernel, "spread_z", message(), back, bf16(z_table().T))


def shards(input_field, cotangent, weights):
    planes = outer(analyse(input_field, cotangent))
    spec = inner(sum_z(planes))
    back, chan = mix(spec, weights)
    back = inner(back)
    zback = outer(spread_z(back))
    return synthesize(zback, chan)


def solution(mesh):
    fields = P("blk", "space", None, None)
    modes = P("space", "blk", None, None, None, None)
    return jax.shard_map(
        shards,
        mesh=mesh,
        in_specs=(fields, fields, modes),
        out_specs=(fields, fields, modes),
        check_vma=False,
    )
```

```python
import math

import jax
import jax.numpy as jnp
import numpy as np
from jax import lax
from jax.experimental import pallas as pl
from jax.experimental.pallas import tpu as pltpu
from jax.sharding import PartitionSpec as P

NX = 96
NY = 192
NZ = 96
MX = 16
MY = 32
MZ = 8
CHANS = 4
CELLS = 6
N_SPACE = 16
N_BLK = 32
PAIR = 2
N_LINE = N_BLK // PAIR
QS = MY // PAIR
ROWS = 16
USED = CHANS // 2 * CELLS
LANES = 128
HALF = LANES // 2
MODES = PAIR * 2 * MZ
FORWARD = 1.0 / math.sqrt(NX * NY * NZ)
SYNTH = 1.0 / math.sqrt(MX * MY * MZ)
VMEM_LIMIT = 48 * 1024 * 1024
LEAD_X = 2
LEAD_Z = 5
LEAD_LINE = 9
F32 = jnp.float32
BF16 = jnp.bfloat16


OUTER = [
    ((LEAD_Z + z) % 8 % 2, (LEAD_X + x) % 4 * 4 + (LEAD_Z + z) % 8 // 2) for x in range(4) for z in range(8)
]
PLACE = {member: place for place, member in enumerate(OUTER)}


def freqs(count):
    index = np.arange(count)
    return np.where(index < count // 2, index, index - count)


def phases(frequencies, length):
    product = (frequencies[:, None] * np.arange(length)[None, :]) % length
    angles = product.astype(np.float32) * np.float32(2.0 * math.pi / length)
    return np.cos(angles).astype(np.float32), np.sin(angles).astype(np.float32)


def bf16(table):
    return jnp.asarray(table.astype(BF16))


def y_analysis():
    cosines, sines = (v.T.reshape(NY, PAIR, QS) for v in phases(freqs(MY), NY))
    table = np.zeros((2, 2, NY, PAIR, 2, 2, QS), np.float32)
    for h in range(2):
        table[h, 0, :, :, h, 0] = cosines
        table[h, 0, :, :, h, 1] = -sines
        table[h, 1, :, :, h, 0] = -sines
        table[h, 1, :, :, h, 1] = -cosines
    return bf16(table.reshape(2, 2, NY, LANES))


def x_analysis():
    cosines, sines = phases(freqs(MX), NX)
    return bf16(np.concatenate([cosines, sines], 0))


def z_table():
    cosines, sines = (v.reshape(MZ, N_SPACE, CELLS) for v in phases(np.arange(MZ), NZ))
    table = np.zeros((2, PAIR, 2, MZ, PAIR, N_SPACE, ROWS), np.float32)
    for pair in range(PAIR):
        for cl in range(2):
            cells = slice(cl * CELLS, (cl + 1) * CELLS)
            table[0, pair, cl, :, pair, :, cells] = cosines
            table[1, pair, cl, :, pair, :, cells] = sines
    table = table.reshape(2 * MODES, PAIR * N_SPACE, ROWS)[:, [pair * N_SPACE + space for pair, space in OUTER]]
    return table.reshape(2 * MODES, PAIR * N_SPACE * ROWS)


def x_synthesis():
    cosines, sines = phases(freqs(MX), NX)
    return bf16(np.concatenate([cosines.T, sines.T], 1))


def y_synthesis():
    cosines, sines = (v.reshape(PAIR, QS, NY) for v in phases(freqs(MY), NY))
    table = np.zeros((2, PAIR, 2, 2, QS, NY), np.float32)
    for h in range(2):
        table[h, :, h, 0] = cosines
        table[h, :, h, 1] = -sines
    return bf16(table.reshape(2, LANES, NY))


def dot(a, b):
    return jnp.dot(a, b, preferred_element_type=F32)


def dot_first(a, b):
    return lax.dot_general(a, b, (((0,), (0,)), ((), ())), preferred_element_type=F32)


def dot_last(a, b):
    return lax.dot_general(a, b, (((1,), (1,)), ((), ())), preferred_element_type=F32)


def index(shape, dim):
    return lax.broadcasted_iota(jnp.int32, shape, dim)


def times_minus_i(a):
    real = index(a.shape, 1) // QS % 2 == 0
    return jnp.where(real, pltpu.roll(a, LANES - QS, 1), -pltpu.roll(a, QS, 1))


def times_i(a):
    real = index(a.shape, 1) // QS % 2 == 0
    return jnp.where(real, -pltpu.roll(a, LANES - QS, 1), pltpu.roll(a, QS, 1))


def low_halves(a, b):
    return jnp.where(index(a.shape, 1) < HALF, a, pltpu.roll(b, HALF, 1))


def high_halves(a, b):
    return jnp.where(index(a.shape, 1) < HALF, pltpu.roll(a, HALF, 1), b)


def analyse_kernel(f_hbm, g_hbm, y_hbm, x_hbm, out_ref, f_ref, g_ref, y_ref, x_ref, sums, planes, sems):
    copies = [pltpu.make_async_copy(x_hbm, x_ref, sems.at[1])]
    for c in range(CHANS):
        copies.append(pltpu.make_async_copy(f_hbm.at[c], f_ref.at[c], sems.at[2 + 2 * c]))
        copies.append(pltpu.make_async_copy(g_hbm.at[c], g_ref.at[c], sems.at[3 + 2 * c]))
    copies.append(pltpu.make_async_copy(y_hbm, y_ref, sems.at[0]))
    for copy in copies:
        copy.start()
    for ch in range(2):
        start = (ch * ROWS + USED) * MX
        planes[start : start + (ROWS - USED) * MX, :] = jnp.zeros(((ROWS - USED) * MX, LANES), F32)
    copies[0].wait()
    for c in range(CHANS):
        copies[1 + 2 * c].wait()
        copies[2 + 2 * c].wait()
        for h, v in enumerate((f_ref, g_ref)):
            for z in range(CELLS):
                part = dot(x_ref[...], v[c, z]).astype(BF16)
                start = (c * CELLS + z) * MX
                for r in range(2):
                    sums[h, r, start : start + MX, :] = part[r * MX : (r + 1) * MX]
    copies[-1].wait()
    for ch in range(2):
        half = slice(ch * USED * MX, (ch + 1) * USED * MX)
        total = 0.0
        for h in range(2):
            for r in range(2):
                total = total + dot(sums[h, r, half], y_ref[h, r])
        start = ch * ROWS * MX
        planes[start : start + USED * MX, :] = total
    for p in range(MX):
        first = planes[pl.ds(p, ROWS, stride=MX), :]
        second = planes[pl.ds(ROWS * MX + p, ROWS, stride=MX), :]
        out_ref[PLACE[0, p]] = low_halves(first, second).astype(BF16)
        out_ref[PLACE[1, p]] = high_halves(first, second).astype(BF16)


def in_hbm(values):
    return pltpu.with_memory_space_constraint(values, pltpu.HBM)


def message():
    return jax.ShapeDtypeStruct((PAIR * N_SPACE, ROWS, LANES), BF16)


def small_message():
    return jax.ShapeDtypeStruct((2 * N_LINE, LANES), F32)


def field_buffer():
    return pltpu.VMEM((CHANS, CELLS, NX, NY), BF16)


def call(kernel, name, out_shape, *operands, in_specs=None, out_specs=None, scratch=()):
    whole = pl.BlockSpec(memory_space=pltpu.VMEM)
    return pl.pallas_call(
        kernel,
        in_specs=in_specs or [whole] * len(operands),
        out_specs=out_specs or jax.tree.map(lambda _: whole, out_shape),
        out_shape=out_shape,
        scratch_shapes=list(scratch),
        compiler_params=pltpu.CompilerParams(vmem_limit_bytes=VMEM_LIMIT),
        name=name,
    )(*operands)


def analyse(field, cotangent):
    return call(
        analyse_kernel,
        "analyse",
        message(),
        *(in_hbm(v) for v in (field, cotangent, y_analysis(), x_analysis())),
        in_specs=[pl.BlockSpec(memory_space=pltpu.HBM)] * 4,
        scratch=[
            field_buffer(),
            field_buffer(),
            pltpu.VMEM((2, 2, NY, LANES), BF16),
            pltpu.VMEM((2 * MX, NX), BF16),
            pltpu.VMEM((2, 2, 4 * CELLS * MX, NY), BF16),
            pltpu.VMEM((2 * ROWS * MX, LANES), F32),
            pltpu.SemaphoreType.DMA((2 + 2 * CHANS,)),
        ],
    )


def line_place(line):
    return (line + N_LINE - LEAD_LINE) % N_LINE


def mode_picker(ch):
    shape = (2 * QS, LANES)
    row, lane = index(shape, 0), index(shape, 1)
    return jnp.where(row == line_place(lane % QS) * 2 + ch, 1.0, 0.0).astype(BF16)


def channel_picker():
    shape = (2 * N_LINE, LANES)
    row, lane = index(shape, 0), index(shape, 1)
    return jnp.where(row == line_place(lane // 4 % N_LINE) * 2 + lane // 2 % 2, 1.0, 0.0).astype(BF16)


def channel_part(shape):
    lane = index(shape, len(shape) - 1)
    return lane // HALF * 2 + lane % 2


def sum_z_kernel(planes_ref, z_ref, out_ref):
    planes = planes_ref[...].reshape(PAIR * N_SPACE * ROWS, LANES)
    sums = dot(z_ref[...], planes)
    spec = sums[:MODES] + times_minus_i(sums[MODES:])
    field = index(spec.shape, 1) // (2 * QS) % 2
    zero = index(spec.shape, 0) % MZ == 0
    scale = jnp.where(field == 0, FORWARD, jnp.where(zero, SYNTH, 2.0 * SYNTH))
    spec = (spec * scale.astype(F32)).astype(BF16).astype(F32)
    shape = (8, MODES, LANES)
    spread = jnp.where(index(shape, 2) // QS == index(shape, 0), spec[None], 0.0).astype(BF16)
    spread = spread.reshape(8 * MODES, LANES)
    first, second = spread[:LANES], spread[LANES:]
    out_ref[...] = dot_last(mode_picker(0), first) + dot_last(mode_picker(1), second)


def mix_kernel(spec_ref, w_ref, back_ref, chan_ref):
    pick = channel_picker()
    wide = dot_first(spec_ref[...].astype(BF16), pick).reshape(4, 4, MZ, LANES)
    part = channel_part((4, MZ, LANES))
    spec = wide[:, 0]
    for j in range(1, 4):
        spec = jnp.where(part == j, wide[:, j], spec)
    chan_ref[...] = spec.reshape(4 * MZ, LANES)
    fr, fi, gr, gi = (spec[i] for i in range(4))
    f = jnp.concatenate([fr, fi], 0).astype(BF16)
    g = jnp.concatenate([gr, gi], 0).astype(BF16)
    own = index((2 * MZ, 2 * LANES), 0) % MZ
    by_f = jnp.zeros((2 * MZ, 2 * LANES), F32)
    by_g = jnp.zeros((2 * MZ, 2 * LANES), F32)
    for k in range(MZ):
        both = w_ref[0, 0, k]
        by_f = jnp.where(own == k, dot_last(f, both.reshape(2 * LANES, LANES)), by_f)
        by_g = jnp.where(own == k, dot(g, jnp.concatenate([both[0], both[1]], 1)), by_g)
    mixed_real = by_f[:MZ, :LANES] - by_f[MZ:, LANES:]
    mixed_imag = by_f[MZ:, :LANES] + by_f[:MZ, LANES:]
    grad_real = by_g[:MZ, :LANES] + by_g[MZ:, LANES:]
    grad_imag = by_g[MZ:, :LANES] - by_g[:MZ, LANES:]
    back = jnp.concatenate([mixed_real, mixed_imag, grad_real, grad_imag], 0)
    back = back.reshape(4, 1, MZ, LANES)
    shape = (4, 4, MZ, LANES)
    spread = jnp.where(channel_part(shape) == index(shape, 1), back, 0.0).astype(BF16)
    back_ref[...] = dot_last(pick, spread.reshape(LANES, LANES))


def spread_z_kernel(back_ref, z_ref, out_ref):
    back = back_ref[...].astype(BF16)
    owner = index((MODES, LANES), 1) // QS
    spec = jnp.zeros((MODES, LANES), F32)
    for ch in range(2):
        wide = dot_first(back, mode_picker(ch)).reshape(4, MODES, LANES)
        for part in range(4):
            spec = jnp.where(owner == 4 * ch + part, wide[part], spec)
    field = owner // 2 % 2
    zero = index(spec.shape, 0) % MZ == 0
    spec = jnp.where((field == 0) & ~zero, 2.0 * spec, spec)
    stacked = jnp.concatenate([spec, times_i(spec)], 0).astype(BF16)
    lane = index((1, LANES), 1) // (2 * QS) % 2
    scale = jnp.where(lane == 0, SYNTH, FORWARD).astype(F32)
    zback = (dot(z_ref[...], stacked) * scale).astype(BF16)
    out_ref[...] = zback.reshape(PAIR * N_SPACE, ROWS, LANES)


def synthesize_kernel(
    zback_ref, chan_ref, x_ref, y_ref, out_hbm, grad_hbm, wgrad_hbm, out_ref, grad_ref, wgrad_ref, planes, mids, sems
):
    copies = []

    def send(source, target):
        copy = pltpu.make_async_copy(source, target, sems.at[len(copies)])
        copy.start()
        copies.append(copy)

    for place, (pair, space) in enumerate(OUTER):
        start = (pair * N_SPACE + space) * ROWS
        planes[start : start + ROWS, :] = zback_ref[place].astype(F32)
    columns = chan_ref[2 * MZ :, :].T.astype(BF16)
    fr, fi = chan_ref[:MZ, :], chan_ref[MZ : 2 * MZ, :]
    pairs = jnp.concatenate([jnp.concatenate([fr, -fi], 1), jnp.concatenate([fi, fr], 1)], 0)
    own = index(pairs.shape, 0) % MZ

    for k in range(MZ):
        both = dot(columns, jnp.where(own == k, pairs, 0.0).astype(BF16))
        wgrad_ref[k, 0] = both[:, :LANES]
        wgrad_ref[k, 1] = both[:, LANES:]
    send(wgrad_ref, wgrad_hbm.at[0, 0])

    def turned(c, z):
        row = c % 2 * CELLS + z
        first = planes[pl.ds(row, MX, stride=ROWS), :]
        second = planes[pl.ds(MX * ROWS + row, MX, stride=ROWS), :]
        plane = low_halves(first, second) if c < 2 else high_halves(first, second)
        return jnp.concatenate([plane, times_i(plane)], 0).astype(BF16)

    def x_part(c):
        for z in range(0, CELLS, 2):
            stacked = jnp.concatenate([turned(c, z), turned(c, z + 1)], 1)
            both = dot(x_ref[...], stacked).astype(BF16)
            mids[c, z * NX : (z + 1) * NX, :] = both[:, :LANES]
            mids[c, (z + 1) * NX : (z + 2) * NX, :] = both[:, LANES:]

    def y_part(c):
        both = mids[c]
        for i, (buffer, target) in enumerate(((out_ref, out_hbm), (grad_ref, grad_hbm))):
            buffer[c] = dot(both, y_ref[i]).astype(BF16).reshape(CELLS, NX, NY)
            send(buffer.at[c], target.at[c])

    x_part(0)
    for c in range(CHANS):
        if c + 1 < CHANS:
            x_part(c + 1)
        y_part(c)
    for copy in copies:
        copy.wait()


def synthesize(zback, chan):
    shape = jax.ShapeDtypeStruct((CHANS, CELLS, NX, NY), BF16)
    wgrad = (MZ, 2, LANES, LANES)
    return call(
        synthesize_kernel,
        "synthesize",
        (shape, shape, jax.ShapeDtypeStruct((1, 1) + wgrad, F32)),
        zback,
        chan,
        x_synthesis(),
        y_synthesis(),
        out_specs=(pl.BlockSpec(memory_space=pltpu.HBM),) * 3,
        scratch=[
            field_buffer(),
            field_buffer(),
            pltpu.VMEM(wgrad, F32),
            pltpu.VMEM((PAIR * N_SPACE * ROWS, LANES), F32),
            pltpu.VMEM((CHANS, CELLS * NX, LANES), BF16),
            pltpu.SemaphoreType.DMA((2 * CHANS + 1,)),
        ],
    )


def outer(values):
    groups = [[(pair * N_LINE + line) * N_SPACE + space for pair, space in OUTER] for line in range(N_LINE)]
    return lax.all_to_all(values, ("blk", "space"), 0, 0, tiled=True, axis_index_groups=groups)


def inner(values):
    lines = [(LEAD_LINE + place) % N_LINE for place in range(N_LINE)]
    groups = [[pair * N_LINE + line for line in lines] for pair in range(PAIR)]
    values = values.reshape(N_LINE, 2, LANES)
    values = lax.all_to_all(values, "blk", 0, 0, tiled=True, axis_index_groups=groups)
    return values.reshape(2 * N_LINE, LANES)


def sum_z(planes):
    return call(sum_z_kernel, "sum_z", small_message(), planes, bf16(z_table()))


def mix(spec, weights):
    return call(mix_kernel, "mix", (small_message(), small_message()), spec, weights)


def spread_z(back):
    return call(spread_z_kernel, "spread_z", message(), back, bf16(z_table().T))


def shards(input_field, cotangent, weights):
    planes = outer(analyse(input_field, cotangent))
    spec = inner(sum_z(planes))
    back, chan = mix(spec, weights)
    back = inner(back)
    zback = outer(spread_z(back))
    return synthesize(zback, chan)


def solution(mesh):
    fields = P("blk", "space", None, None)
    modes = P("space", "blk", None, None, None, None)
    return jax.shard_map(
        shards,
        mesh=mesh,
        in_specs=(fields, fields, modes),
        out_specs=(fields, fields, modes),
        check_vma=False,
    )
```

```python
import math

import jax
import jax.numpy as jnp
import numpy as np
from jax import lax
from jax.experimental import pallas as pl
from jax.experimental.pallas import tpu as pltpu
from jax.sharding import PartitionSpec as P

NX = 96
NY = 192
NZ = 96
MX = 16
MY = 32
MZ = 8
CHANS = 4
CELLS = 6
N_SPACE = 16
N_BLK = 32
PAIR = 2
N_LINE = N_BLK // PAIR
QS = MY // PAIR
ROWS = 16
USED = CHANS // 2 * CELLS
LANES = 128
HALF = LANES // 2
MODES = PAIR * 2 * MZ
FORWARD = 1.0 / math.sqrt(NX * NY * NZ)
SYNTH = 1.0 / math.sqrt(MX * MY * MZ)
VMEM_LIMIT = 48 * 1024 * 1024
FIRST_X = 2
FIRST_Z = 5
LAST_X = 2
LAST_Z = 5
THERE_LINE = 9
BACK_LINE = 9
F32 = jnp.float32
BF16 = jnp.bfloat16


def members(lead_x, lead_z):
    ring = [((lead_x + x) % 4, (lead_z + z) % 8) for x in range(4) for z in range(8)]
    return [(z % 2, 4 * x + z // 2) for x, z in ring]


FIRST = members(FIRST_X, FIRST_Z)
LAST = members(LAST_X, LAST_Z)


def freqs(count):
    index = np.arange(count)
    return np.where(index < count // 2, index, index - count)


def phases(frequencies, length):
    product = (frequencies[:, None] * np.arange(length)[None, :]) % length
    angles = product.astype(np.float32) * np.float32(2.0 * math.pi / length)
    return np.cos(angles).astype(np.float32), np.sin(angles).astype(np.float32)


def bf16(table):
    return jnp.asarray(table.astype(BF16))


def y_analysis():
    cosines, sines = (v.T.reshape(NY, PAIR, 1, QS) for v in phases(freqs(MY), NY))
    table = np.zeros((2, NY, PAIR, 2, 2, QS), np.float32)
    table[0, :, :, :, 0] = cosines
    table[0, :, :, :, 1] = -sines
    table[1, :, :, :, 0] = -sines
    table[1, :, :, :, 1] = -cosines
    return bf16(table.reshape(2, NY, LANES))


def x_analysis():
    cosines, sines = phases(freqs(MX), NX)
    return bf16(np.concatenate([cosines, sines], 0))


def z_table(order):
    cosines, sines = (v.reshape(MZ, N_SPACE, CELLS) for v in phases(np.arange(MZ), NZ))
    table = np.zeros((2, PAIR, 2, MZ, PAIR, N_SPACE, ROWS), np.float32)
    for pair in range(PAIR):
        for cl in range(2):
            cells = slice(cl * CELLS, (cl + 1) * CELLS)
            table[0, pair, cl, :, pair, :, cells] = cosines
            table[1, pair, cl, :, pair, :, cells] = sines
    table = table.reshape(2 * MODES, PAIR * N_SPACE, ROWS)[:, [pair * N_SPACE + space for pair, space in order]]
    return table.reshape(2 * MODES, PAIR * N_SPACE * ROWS)


def x_synthesis():
    cosines, sines = phases(freqs(MX), NX)
    return bf16(np.concatenate([cosines.T, sines.T], 1))


def y_synthesis():
    cosines, sines = (v.reshape(PAIR, QS, NY) for v in phases(freqs(MY), NY))
    table = np.zeros((2, PAIR, 2, 2, QS, NY), np.float32)
    for h in range(2):
        table[h, :, h, 0] = cosines
        table[h, :, h, 1] = -sines
    return bf16(table.reshape(2, LANES, NY))


def dot(a, b):
    return jnp.dot(a, b, preferred_element_type=F32)


def dot_first(a, b):
    return lax.dot_general(a, b, (((0,), (0,)), ((), ())), preferred_element_type=F32)


def dot_last(a, b):
    return lax.dot_general(a, b, (((1,), (1,)), ((), ())), preferred_element_type=F32)


def index(shape, dim):
    return lax.broadcasted_iota(jnp.int32, shape, dim)


def times_minus_i(a):
    real = index(a.shape, 1) // QS % 2 == 0
    return jnp.where(real, pltpu.roll(a, LANES - QS, 1), -pltpu.roll(a, QS, 1))


def times_i(a):
    real = index(a.shape, 1) // QS % 2 == 0
    return jnp.where(real, -pltpu.roll(a, LANES - QS, 1), pltpu.roll(a, QS, 1))


def low_halves(a, b):
    return jnp.where(index(a.shape, 1) < HALF, a, pltpu.roll(b, HALF, 1))


def high_halves(a, b):
    return jnp.where(index(a.shape, 1) < HALF, pltpu.roll(a, HALF, 1), b)


def analyse_kernel(f_hbm, g_hbm, y_hbm, x_hbm, out_ref, f_ref, g_ref, y_ref, x_ref, sums, planes, sems):
    copies = [pltpu.make_async_copy(x_hbm, x_ref, sems.at[1])]
    for c in range(CHANS):
        copies.append(pltpu.make_async_copy(f_hbm.at[c], f_ref.at[c], sems.at[2 + 2 * c]))
        copies.append(pltpu.make_async_copy(g_hbm.at[c], g_ref.at[c], sems.at[3 + 2 * c]))
    copies.append(pltpu.make_async_copy(y_hbm, y_ref, sems.at[0]))
    for copy in copies:
        copy.start()
    for ch in range(2):
        start = (ch * ROWS + USED) * MX
        planes[start : start + (ROWS - USED) * MX, :] = jnp.zeros(((ROWS - USED) * MX, LANES), F32)
    copies[0].wait()
    for c in range(CHANS):
        copies[1 + 2 * c].wait()
        copies[2 + 2 * c].wait()
        for z in range(CELLS):
            for h, v in enumerate((f_ref, g_ref)):
                part = dot(x_ref[...], v[c, z]).astype(BF16)
                start = ((h * CHANS + c) * CELLS + z) * MX
                for r in range(2):
                    sums[r, start : start + MX, :] = part[r * MX : (r + 1) * MX]
    copies[-1].wait()
    both = dot(sums[0], y_ref[0]) + dot(sums[1], y_ref[1])
    half = 2 * USED * MX
    total = jnp.where(index((half, LANES), 1) // (2 * QS) % 2 == 0, both[:half], both[half:])
    for ch in range(2):
        start = ch * ROWS * MX
        planes[start : start + USED * MX, :] = total[ch * USED * MX : (ch + 1) * USED * MX]
    for p in range(MX):
        first = planes[pl.ds(p, ROWS, stride=MX), :]
        second = planes[pl.ds(ROWS * MX + p, ROWS, stride=MX), :]
        out_ref[FIRST.index((0, p))] = low_halves(first, second).astype(BF16)
        out_ref[FIRST.index((1, p))] = high_halves(first, second).astype(BF16)


def in_hbm(values):
    return pltpu.with_memory_space_constraint(values, pltpu.HBM)


def message():
    return jax.ShapeDtypeStruct((PAIR * N_SPACE, ROWS, LANES), BF16)


def small_message():
    return jax.ShapeDtypeStruct((2 * N_LINE, LANES), F32)


def field_buffer():
    return pltpu.VMEM((CHANS, CELLS, NX, NY), BF16)


def call(kernel, name, out_shape, *operands, in_specs=None, out_specs=None, scratch=()):
    whole = pl.BlockSpec(memory_space=pltpu.VMEM)
    return pl.pallas_call(
        kernel,
        in_specs=in_specs or [whole] * len(operands),
        out_specs=out_specs or jax.tree.map(lambda _: whole, out_shape),
        out_shape=out_shape,
        scratch_shapes=list(scratch),
        compiler_params=pltpu.CompilerParams(vmem_limit_bytes=VMEM_LIMIT),
        name=name,
    )(*operands)


def analyse(field, cotangent):
    return call(
        analyse_kernel,
        "analyse",
        message(),
        *(in_hbm(v) for v in (field, cotangent, y_analysis(), x_analysis())),
        in_specs=[pl.BlockSpec(memory_space=pltpu.HBM)] * 4,
        scratch=[
            field_buffer(),
            field_buffer(),
            pltpu.VMEM((2, NY, LANES), BF16),
            pltpu.VMEM((2 * MX, NX), BF16),
            pltpu.VMEM((2, 2 * CHANS * CELLS * MX, NY), BF16),
            pltpu.VMEM((2 * ROWS * MX, LANES), F32),
            pltpu.SemaphoreType.DMA((2 + 2 * CHANS,)),
        ],
    )


def line_place(line, lead):
    return (line + N_LINE - lead) % N_LINE


def mode_picker(ch, lead):
    shape = (2 * QS, LANES)
    row, lane = index(shape, 0), index(shape, 1)
    return jnp.where(row == line_place(lane % QS, lead) * 2 + ch, 1.0, 0.0).astype(BF16)


def channel_picker(lead):
    shape = (2 * N_LINE, LANES)
    row, lane = index(shape, 0), index(shape, 1)
    return jnp.where(row == line_place(lane // 4 % N_LINE, lead) * 2 + lane // 2 % 2, 1.0, 0.0).astype(BF16)


def channel_part(shape):
    lane = index(shape, len(shape) - 1)
    return lane // HALF * 2 + lane % 2


def sum_z_kernel(planes_ref, z_ref, out_ref):
    planes = planes_ref[...].reshape(PAIR * N_SPACE * ROWS, LANES)
    sums = dot(z_ref[...], planes)
    spec = sums[:MODES] + times_minus_i(sums[MODES:])
    field = index(spec.shape, 1) // (2 * QS) % 2
    zero = index(spec.shape, 0) % MZ == 0
    scale = jnp.where(field == 0, FORWARD, jnp.where(zero, SYNTH, 2.0 * SYNTH))
    spec = (spec * scale.astype(F32)).astype(BF16).astype(F32)
    shape = (8, MODES, LANES)
    spread = jnp.where(index(shape, 2) // QS == index(shape, 0), spec[None], 0.0).astype(BF16)
    spread = spread.reshape(8 * MODES, LANES)
    first, second = spread[:LANES], spread[LANES:]
    out_ref[...] = dot_last(mode_picker(0, THERE_LINE), first) + dot_last(mode_picker(1, THERE_LINE), second)


def mix_kernel(spec_ref, w_ref, back_ref, chan_ref):
    wide = dot_first(spec_ref[...].astype(BF16), channel_picker(THERE_LINE)).reshape(4, 4, MZ, LANES)
    part = channel_part((4, MZ, LANES))
    spec = wide[:, 0]
    for j in range(1, 4):
        spec = jnp.where(part == j, wide[:, j], spec)
    chan_ref[...] = spec.reshape(4 * MZ, LANES)
    fr, fi, gr, gi = (spec[i] for i in range(4))
    f = jnp.concatenate([fr, fi], 0).astype(BF16)
    g = jnp.concatenate([gr, gi], 0).astype(BF16)
    own = index((2 * MZ, 2 * LANES), 0) % MZ
    by_f = jnp.zeros((2 * MZ, 2 * LANES), F32)
    by_g = jnp.zeros((2 * MZ, 2 * LANES), F32)
    for k in range(MZ):
        both = w_ref[0, 0, k]
        by_f = jnp.where(own == k, dot_last(f, both.reshape(2 * LANES, LANES)), by_f)
        by_g = jnp.where(own == k, dot(g, jnp.concatenate([both[0], both[1]], 1)), by_g)
    mixed_real = by_f[:MZ, :LANES] - by_f[MZ:, LANES:]
    mixed_imag = by_f[MZ:, :LANES] + by_f[:MZ, LANES:]
    grad_real = by_g[:MZ, :LANES] + by_g[MZ:, LANES:]
    grad_imag = by_g[MZ:, :LANES] - by_g[:MZ, LANES:]
    back = jnp.concatenate([mixed_real, mixed_imag, grad_real, grad_imag], 0)
    back = back.reshape(4, 1, MZ, LANES)
    shape = (4, 4, MZ, LANES)
    spread = jnp.where(channel_part(shape) == index(shape, 1), back, 0.0).astype(BF16)
    back_ref[...] = dot_last(channel_picker(BACK_LINE), spread.reshape(LANES, LANES))


def spread_z_kernel(back_ref, z_ref, out_ref):
    back = back_ref[...].astype(BF16)
    owner = index((MODES, LANES), 1) // QS
    spec = jnp.zeros((MODES, LANES), F32)
    for ch in range(2):
        wide = dot_first(back, mode_picker(ch, BACK_LINE)).reshape(4, MODES, LANES)
        for part in range(4):
            spec = jnp.where(owner == 4 * ch + part, wide[part], spec)
    field = owner // 2 % 2
    zero = index(spec.shape, 0) % MZ == 0
    spec = jnp.where((field == 0) & ~zero, 2.0 * spec, spec)
    stacked = jnp.concatenate([spec, times_i(spec)], 0).astype(BF16)
    lane = index((1, LANES), 1) // (2 * QS) % 2
    scale = jnp.where(lane == 0, SYNTH, FORWARD).astype(F32)
    zback = (dot(z_ref[...], stacked) * scale).astype(BF16)
    out_ref[...] = zback.reshape(PAIR * N_SPACE, ROWS, LANES)


def synthesize_kernel(
    zback_ref, chan_ref, x_ref, y_ref, out_hbm, grad_hbm, wgrad_hbm, out_ref, grad_ref, wgrad_ref, planes, mids, sems
):
    copies = []

    def send(source, target):
        copy = pltpu.make_async_copy(source, target, sems.at[len(copies)])
        copy.start()
        copies.append(copy)

    for place, (pair, space) in enumerate(LAST):
        start = (pair * N_SPACE + space) * ROWS
        planes[start : start + ROWS, :] = zback_ref[place].astype(F32)
    columns = chan_ref[2 * MZ :, :].T.astype(BF16)
    fr, fi = chan_ref[:MZ, :], chan_ref[MZ : 2 * MZ, :]
    pairs = jnp.concatenate([jnp.concatenate([fr, -fi], 1), jnp.concatenate([fi, fr], 1)], 0)
    own = index(pairs.shape, 0) % MZ

    for k in range(MZ):
        both = dot(columns, jnp.where(own == k, pairs, 0.0).astype(BF16))
        wgrad_ref[k, 0] = both[:, :LANES]
        wgrad_ref[k, 1] = both[:, LANES:]
    send(wgrad_ref, wgrad_hbm.at[0, 0])

    def turned(c, z):
        row = c % 2 * CELLS + z
        first = planes[pl.ds(row, MX, stride=ROWS), :]
        second = planes[pl.ds(MX * ROWS + row, MX, stride=ROWS), :]
        plane = low_halves(first, second) if c < 2 else high_halves(first, second)
        return jnp.concatenate([plane, times_i(plane)], 0).astype(BF16)

    def x_part(c):
        for z in range(0, CELLS, 2):
            stacked = jnp.concatenate([turned(c, z), turned(c, z + 1)], 1)
            both = dot(x_ref[...], stacked).astype(BF16)
            mids[c, z * NX : (z + 1) * NX, :] = both[:, :LANES]
            mids[c, (z + 1) * NX : (z + 2) * NX, :] = both[:, LANES:]

    def y_part(c):
        both = mids[c]
        for i, (buffer, target) in enumerate(((out_ref, out_hbm), (grad_ref, grad_hbm))):
            buffer[c] = dot(both, y_ref[i]).astype(BF16).reshape(CELLS, NX, NY)
            send(buffer.at[c], target.at[c])

    x_part(0)
    for c in range(CHANS):
        if c + 1 < CHANS:
            x_part(c + 1)
        y_part(c)
    for copy in copies:
        copy.wait()


def synthesize(zback, chan):
    shape = jax.ShapeDtypeStruct((CHANS, CELLS, NX, NY), BF16)
    wgrad = (MZ, 2, LANES, LANES)
    return call(
        synthesize_kernel,
        "synthesize",
        (shape, shape, jax.ShapeDtypeStruct((1, 1) + wgrad, F32)),
        zback,
        chan,
        x_synthesis(),
        y_synthesis(),
        out_specs=(pl.BlockSpec(memory_space=pltpu.HBM),) * 3,
        scratch=[
            field_buffer(),
            field_buffer(),
            pltpu.VMEM(wgrad, F32),
            pltpu.VMEM((PAIR * N_SPACE * ROWS, LANES), F32),
            pltpu.VMEM((CHANS, CELLS * NX, LANES), BF16),
            pltpu.SemaphoreType.DMA((2 * CHANS + 1,)),
        ],
    )


def outer(values, order):
    groups = [[(pair * N_LINE + line) * N_SPACE + space for pair, space in order] for line in range(N_LINE)]
    return lax.all_to_all(values, ("blk", "space"), 0, 0, tiled=True, axis_index_groups=groups)


def inner(values, lead):
    lines = [(lead + place) % N_LINE for place in range(N_LINE)]
    groups = [[pair * N_LINE + line for line in lines] for pair in range(PAIR)]
    values = values.reshape(N_LINE, 2, LANES)
    values = lax.all_to_all(values, "blk", 0, 0, tiled=True, axis_index_groups=groups)
    return values.reshape(2 * N_LINE, LANES)


def sum_z(planes):
    return call(sum_z_kernel, "sum_z", small_message(), planes, bf16(z_table(FIRST)))


def mix(spec, weights):
    return call(mix_kernel, "mix", (small_message(), small_message()), spec, weights)


def spread_z(back):
    return call(spread_z_kernel, "spread_z", message(), back, bf16(z_table(LAST).T))


def shards(input_field, cotangent, weights):
    planes = outer(analyse(input_field, cotangent), FIRST)
    spec = inner(sum_z(planes), THERE_LINE)
    back, chan = mix(spec, weights)
    back = inner(back, BACK_LINE)
    zback = outer(spread_z(back), LAST)
    return synthesize(zback, chan)


def solution(mesh):
    fields = P("blk", "space", None, None)
    modes = P("space", "blk", None, None, None, None)
    return jax.shard_map(
        shards,
        mesh=mesh,
        in_specs=(fields, fields, modes),
        out_specs=(fields, fields, modes),
        check_vma=False,
    )
```

```python
import math

import jax
import jax.numpy as jnp
import numpy as np
from jax import lax
from jax.experimental import pallas as pl
from jax.experimental.pallas import tpu as pltpu
from jax.sharding import PartitionSpec as P

NX = 96
NY = 192
NZ = 96
MX = 16
MY = 32
MZ = 8
CHANS = 4
CELLS = 6
N_SPACE = 16
N_BLK = 32
PAIR = 2
N_LINE = N_BLK // PAIR
QS = MY // PAIR
ROWS = 16
USED = CHANS // 2 * CELLS
STEP = 4
PARTS = USED // STEP
LANES = 128
HALF = LANES // 2
MODES = PAIR * 2 * MZ
FORWARD = 1.0 / math.sqrt(NX * NY * NZ)
SYNTH = 1.0 / math.sqrt(MX * MY * MZ)
VMEM_LIMIT = 48 * 1024 * 1024
FIRST_X = 2
FIRST_Z = 5
LAST_X = 2
LAST_Z = 5
THERE_LINE = 9
BACK_LINE = 9
F32 = jnp.float32
BF16 = jnp.bfloat16


def members(lead_x, lead_z):
    ring = [((lead_x + x) % 4, (lead_z + z) % 8) for x in range(4) for z in range(8)]
    return [(z % 2, 4 * x + z // 2) for x, z in ring]


FIRST = members(FIRST_X, FIRST_Z)
LAST = members(LAST_X, LAST_Z)


def freqs(count):
    index = np.arange(count)
    return np.where(index < count // 2, index, index - count)


def phases(frequencies, length):
    product = (frequencies[:, None] * np.arange(length)[None, :]) % length
    angles = product.astype(np.float32) * np.float32(2.0 * math.pi / length)
    return np.cos(angles).astype(np.float32), np.sin(angles).astype(np.float32)


def bf16(table):
    return jnp.asarray(table.astype(BF16))


def y_analysis():
    cosines, sines = (v.T.reshape(NY, PAIR, 1, QS) for v in phases(freqs(MY), NY))
    table = np.zeros((2, NY, PAIR, 2, 2, QS), np.float32)
    table[0, :, :, :, 0] = cosines
    table[0, :, :, :, 1] = -sines
    table[1, :, :, :, 0] = -sines
    table[1, :, :, :, 1] = -cosines
    return bf16(table.reshape(2, NY, LANES))


def x_analysis():
    cosines, sines = phases(freqs(MX), NX)
    return bf16(np.concatenate([cosines, sines], 0))


def z_table(order):
    cosines, sines = (v.reshape(MZ, N_SPACE, CELLS) for v in phases(np.arange(MZ), NZ))
    table = np.zeros((2, PAIR, 2, MZ, PAIR, N_SPACE, USED), np.float32)
    for pair in range(PAIR):
        for cl in range(2):
            cells = slice(cl * CELLS, (cl + 1) * CELLS)
            table[0, pair, cl, :, pair, :, cells] = cosines
            table[1, pair, cl, :, pair, :, cells] = sines
    table = table.reshape(2 * MODES, PAIR * N_SPACE, USED)[:, [pair * N_SPACE + space for pair, space in order]]
    return table.reshape(2 * MODES, PAIR * N_SPACE * USED)


def x_synthesis():
    cosines, sines = phases(freqs(MX), NX)
    return bf16(np.concatenate([cosines.T, sines.T], 1))


def y_synthesis():
    cosines, sines = (v.reshape(PAIR, QS, NY) for v in phases(freqs(MY), NY))
    table = np.zeros((2, PAIR, 2, 2, QS, NY), np.float32)
    for h in range(2):
        table[h, :, h, 0] = cosines
        table[h, :, h, 1] = -sines
    return bf16(table.reshape(2, LANES, NY))


def dot(a, b):
    return jnp.dot(a, b, preferred_element_type=F32)


def dot_first(a, b):
    return lax.dot_general(a, b, (((0,), (0,)), ((), ())), preferred_element_type=F32)


def dot_last(a, b):
    return lax.dot_general(a, b, (((1,), (1,)), ((), ())), preferred_element_type=F32)


def index(shape, dim):
    return lax.broadcasted_iota(jnp.int32, shape, dim)


def times_minus_i(a):
    real = index(a.shape, 1) // QS % 2 == 0
    return jnp.where(real, pltpu.roll(a, LANES - QS, 1), -pltpu.roll(a, QS, 1))


def times_i(a):
    real = index(a.shape, 1) // QS % 2 == 0
    return jnp.where(real, -pltpu.roll(a, LANES - QS, 1), pltpu.roll(a, QS, 1))


def low_halves(a, b):
    return jnp.where(index(a.shape, 1) < HALF, a, pltpu.roll(b, HALF, 1))


def high_halves(a, b):
    return jnp.where(index(a.shape, 1) < HALF, pltpu.roll(a, HALF, 1), b)


def analyse_kernel(f_hbm, g_hbm, y_hbm, x_hbm, out_ref, f_ref, g_ref, y_ref, x_ref, sums, planes, sems):
    copies = [pltpu.make_async_copy(x_hbm, x_ref, sems.at[1])]
    for c in range(CHANS):
        copies.append(pltpu.make_async_copy(f_hbm.at[c], f_ref.at[c], sems.at[2 + 2 * c]))
        copies.append(pltpu.make_async_copy(g_hbm.at[c], g_ref.at[c], sems.at[3 + 2 * c]))
    copies.append(pltpu.make_async_copy(y_hbm, y_ref, sems.at[0]))
    for copy in copies:
        copy.start()
    copies[0].wait()
    for c in range(CHANS):
        copies[1 + 2 * c].wait()
        copies[2 + 2 * c].wait()
        for z in range(CELLS):
            for h, v in enumerate((f_ref, g_ref)):
                part = dot(x_ref[...], v[c, z]).astype(BF16)
                start = ((h * CHANS + c) * CELLS + z) * MX
                for r in range(2):
                    sums[r, start : start + MX, :] = part[r * MX : (r + 1) * MX]
    copies[-1].wait()
    both = dot(sums[0], y_ref[0]) + dot(sums[1], y_ref[1])
    half = 2 * USED * MX
    total = jnp.where(index((half, LANES), 1) // (2 * QS) % 2 == 0, both[:half], both[half:])
    for ch in range(2):
        start = ch * ROWS * MX
        planes[start : start + USED * MX, :] = total[ch * USED * MX : (ch + 1) * USED * MX]
    for p in range(MX):
        for part in range(PARTS):
            first = planes[pl.ds(part * STEP * MX + p, STEP, stride=MX), :]
            second = planes[pl.ds((ROWS + part * STEP) * MX + p, STEP, stride=MX), :]
            out_ref[FIRST.index((0, p)), part] = low_halves(first, second).astype(BF16)
            out_ref[FIRST.index((1, p)), part] = high_halves(first, second).astype(BF16)


def in_hbm(values):
    return pltpu.with_memory_space_constraint(values, pltpu.HBM)


def message():
    return jax.ShapeDtypeStruct((PAIR * N_SPACE, PARTS, STEP, LANES), BF16)


def small_message():
    return jax.ShapeDtypeStruct((2 * N_LINE, LANES), F32)


def field_buffer():
    return pltpu.VMEM((CHANS, CELLS, NX, NY), BF16)


def call(kernel, name, out_shape, *operands, in_specs=None, out_specs=None, scratch=()):
    whole = pl.BlockSpec(memory_space=pltpu.VMEM)
    return pl.pallas_call(
        kernel,
        in_specs=in_specs or [whole] * len(operands),
        out_specs=out_specs or jax.tree.map(lambda _: whole, out_shape),
        out_shape=out_shape,
        scratch_shapes=list(scratch),
        compiler_params=pltpu.CompilerParams(vmem_limit_bytes=VMEM_LIMIT),
        name=name,
    )(*operands)


def analyse(field, cotangent):
    return call(
        analyse_kernel,
        "analyse",
        message(),
        *(in_hbm(v) for v in (field, cotangent, y_analysis(), x_analysis())),
        in_specs=[pl.BlockSpec(memory_space=pltpu.HBM)] * 4,
        scratch=[
            field_buffer(),
            field_buffer(),
            pltpu.VMEM((2, NY, LANES), BF16),
            pltpu.VMEM((2 * MX, NX), BF16),
            pltpu.VMEM((2, 2 * CHANS * CELLS * MX, NY), BF16),
            pltpu.VMEM((2 * ROWS * MX, LANES), F32),
            pltpu.SemaphoreType.DMA((2 + 2 * CHANS,)),
        ],
    )


def line_place(line, lead):
    return (line + N_LINE - lead) % N_LINE


def mode_picker(ch, lead):
    shape = (2 * QS, LANES)
    row, lane = index(shape, 0), index(shape, 1)
    return jnp.where(row == line_place(lane % QS, lead) * 2 + ch, 1.0, 0.0).astype(BF16)


def channel_picker(lead):
    shape = (2 * N_LINE, LANES)
    row, lane = index(shape, 0), index(shape, 1)
    return jnp.where(row == line_place(lane // 4 % N_LINE, lead) * 2 + lane // 2 % 2, 1.0, 0.0).astype(BF16)


def channel_part(shape):
    lane = index(shape, len(shape) - 1)
    return lane // HALF * 2 + lane % 2


def sum_z_kernel(planes_ref, z_ref, out_ref, planes):
    for place in range(PAIR * N_SPACE):
        for part in range(PARTS):
            start = place * USED + part * STEP
            planes[start : start + STEP, :] = planes_ref[place, part].astype(F32)
    sums = dot(z_ref[...], planes[...].astype(BF16))
    spec = sums[:MODES] + times_minus_i(sums[MODES:])
    field = index(spec.shape, 1) // (2 * QS) % 2
    zero = index(spec.shape, 0) % MZ == 0
    scale = jnp.where(field == 0, FORWARD, jnp.where(zero, SYNTH, 2.0 * SYNTH))
    spec = (spec * scale.astype(F32)).astype(BF16).astype(F32)
    shape = (8, MODES, LANES)
    spread = jnp.where(index(shape, 2) // QS == index(shape, 0), spec[None], 0.0).astype(BF16)
    spread = spread.reshape(8 * MODES, LANES)
    first, second = spread[:LANES], spread[LANES:]
    out_ref[...] = dot_last(mode_picker(0, THERE_LINE), first) + dot_last(mode_picker(1, THERE_LINE), second)


def mix_kernel(spec_ref, w_ref, back_ref, chan_ref):
    wide = dot_first(spec_ref[...].astype(BF16), channel_picker(THERE_LINE)).reshape(4, 4, MZ, LANES)
    part = channel_part((4, MZ, LANES))
    spec = wide[:, 0]
    for j in range(1, 4):
        spec = jnp.where(part == j, wide[:, j], spec)
    chan_ref[...] = spec.reshape(4 * MZ, LANES)
    fr, fi, gr, gi = (spec[i] for i in range(4))
    f = jnp.concatenate([fr, fi], 0).astype(BF16)
    g = jnp.concatenate([gr, gi], 0).astype(BF16)
    own = index((2 * MZ, 2 * LANES), 0) % MZ
    by_f = jnp.zeros((2 * MZ, 2 * LANES), F32)
    by_g = jnp.zeros((2 * MZ, 2 * LANES), F32)
    for k in range(MZ):
        both = w_ref[0, 0, k]
        by_f = jnp.where(own == k, dot_last(f, both.reshape(2 * LANES, LANES)), by_f)
        by_g = jnp.where(own == k, dot(g, jnp.concatenate([both[0], both[1]], 1)), by_g)
    mixed_real = by_f[:MZ, :LANES] - by_f[MZ:, LANES:]
    mixed_imag = by_f[MZ:, :LANES] + by_f[:MZ, LANES:]
    grad_real = by_g[:MZ, :LANES] + by_g[MZ:, LANES:]
    grad_imag = by_g[MZ:, :LANES] - by_g[:MZ, LANES:]
    back = jnp.concatenate([mixed_real, mixed_imag, grad_real, grad_imag], 0)
    back = back.reshape(4, 1, MZ, LANES)
    shape = (4, 4, MZ, LANES)
    spread = jnp.where(channel_part(shape) == index(shape, 1), back, 0.0).astype(BF16)
    back_ref[...] = dot_last(channel_picker(BACK_LINE), spread.reshape(LANES, LANES))


def spread_z_kernel(back_ref, z_ref, out_ref):
    back = back_ref[...].astype(BF16)
    owner = index((MODES, LANES), 1) // QS
    spec = jnp.zeros((MODES, LANES), F32)
    for ch in range(2):
        wide = dot_first(back, mode_picker(ch, BACK_LINE)).reshape(4, MODES, LANES)
        for part in range(4):
            spec = jnp.where(owner == 4 * ch + part, wide[part], spec)
    field = owner // 2 % 2
    zero = index(spec.shape, 0) % MZ == 0
    spec = jnp.where((field == 0) & ~zero, 2.0 * spec, spec)
    stacked = jnp.concatenate([spec, times_i(spec)], 0).astype(BF16)
    lane = index((1, LANES), 1) // (2 * QS) % 2
    scale = jnp.where(lane == 0, SYNTH, FORWARD).astype(F32)
    zback = dot(z_ref[...], stacked) * scale
    for place in range(PAIR * N_SPACE):
        for part in range(PARTS):
            start = place * USED + part * STEP
            out_ref[place, part] = zback[start : start + STEP].astype(BF16)


def synthesize_kernel(
    zback_ref, chan_ref, x_ref, y_ref, out_hbm, grad_hbm, wgrad_hbm, out_ref, grad_ref, wgrad_ref, planes, mids, sems
):
    copies = []

    def send(source, target):
        copy = pltpu.make_async_copy(source, target, sems.at[len(copies)])
        copy.start()
        copies.append(copy)

    for place, (pair, space) in enumerate(LAST):
        start = (pair * N_SPACE + space) * ROWS
        for part in range(PARTS):
            planes[start + part * STEP : start + (part + 1) * STEP, :] = zback_ref[place, part].astype(F32)
    columns = chan_ref[2 * MZ :, :].T.astype(BF16)
    fr, fi = chan_ref[:MZ, :], chan_ref[MZ : 2 * MZ, :]
    pairs = jnp.concatenate([jnp.concatenate([fr, -fi], 1), jnp.concatenate([fi, fr], 1)], 0)
    own = index(pairs.shape, 0) % MZ

    for k in range(MZ):
        both = dot(columns, jnp.where(own == k, pairs, 0.0).astype(BF16))
        wgrad_ref[k, 0] = both[:, :LANES]
        wgrad_ref[k, 1] = both[:, LANES:]
    send(wgrad_ref, wgrad_hbm.at[0, 0])

    def turned(c, z):
        row = c % 2 * CELLS + z
        first = planes[pl.ds(row, MX, stride=ROWS), :]
        second = planes[pl.ds(MX * ROWS + row, MX, stride=ROWS), :]
        plane = low_halves(first, second) if c < 2 else high_halves(first, second)
        return jnp.concatenate([plane, times_i(plane)], 0).astype(BF16)

    def x_part(c):
        for z in range(0, CELLS, 2):
            stacked = jnp.concatenate([turned(c, z), turned(c, z + 1)], 1)
            both = dot(x_ref[...], stacked).astype(BF16)
            mids[c, z * NX : (z + 1) * NX, :] = both[:, :LANES]
            mids[c, (z + 1) * NX : (z + 2) * NX, :] = both[:, LANES:]

    def y_part(c):
        both = mids[c]
        for i, (buffer, target) in enumerate(((out_ref, out_hbm), (grad_ref, grad_hbm))):
            buffer[c] = dot(both, y_ref[i]).astype(BF16).reshape(CELLS, NX, NY)
            send(buffer.at[c], target.at[c])

    x_part(0)
    for c in range(CHANS):
        if c + 1 < CHANS:
            x_part(c + 1)
        y_part(c)
    for copy in copies:
        copy.wait()


def synthesize(zback, chan):
    shape = jax.ShapeDtypeStruct((CHANS, CELLS, NX, NY), BF16)
    wgrad = (MZ, 2, LANES, LANES)
    return call(
        synthesize_kernel,
        "synthesize",
        (shape, shape, jax.ShapeDtypeStruct((1, 1) + wgrad, F32)),
        zback,
        chan,
        x_synthesis(),
        y_synthesis(),
        out_specs=(pl.BlockSpec(memory_space=pltpu.HBM),) * 3,
        scratch=[
            field_buffer(),
            field_buffer(),
            pltpu.VMEM(wgrad, F32),
            pltpu.VMEM((PAIR * N_SPACE * ROWS, LANES), F32),
            pltpu.VMEM((CHANS, CELLS * NX, LANES), BF16),
            pltpu.SemaphoreType.DMA((2 * CHANS + 1,)),
        ],
    )


def outer(values, order):
    groups = [[(pair * N_LINE + line) * N_SPACE + space for pair, space in order] for line in range(N_LINE)]
    return lax.all_to_all(values, ("blk", "space"), 0, 0, tiled=True, axis_index_groups=groups)


def inner(values, lead):
    lines = [(lead + place) % N_LINE for place in range(N_LINE)]
    groups = [[pair * N_LINE + line for line in lines] for pair in range(PAIR)]
    values = values.reshape(N_LINE, 2, LANES)
    values = lax.all_to_all(values, "blk", 0, 0, tiled=True, axis_index_groups=groups)
    return values.reshape(2 * N_LINE, LANES)


def sum_z(planes):
    return call(sum_z_kernel, "sum_z", small_message(), planes, bf16(z_table(FIRST)), scratch=[pltpu.VMEM((PAIR * N_SPACE * USED, LANES), F32)])


def mix(spec, weights):
    return call(mix_kernel, "mix", (small_message(), small_message()), spec, weights)


def spread_z(back):
    return call(spread_z_kernel, "spread_z", message(), back, bf16(z_table(LAST).T))


def shards(input_field, cotangent, weights):
    planes = outer(analyse(input_field, cotangent), FIRST)
    spec = inner(sum_z(planes), THERE_LINE)
    back, chan = mix(spec, weights)
    back = inner(back, BACK_LINE)
    zback = outer(spread_z(back), LAST)
    return synthesize(zback, chan)


def solution(mesh):
    fields = P("blk", "space", None, None)
    modes = P("space", "blk", None, None, None, None)
    return jax.shard_map(
        shards,
        mesh=mesh,
        in_specs=(fields, fields, modes),
        out_specs=(fields, fields, modes),
        check_vma=False,
    )
```

```python
import math

import jax
import jax.numpy as jnp
import numpy as np
from jax import lax
from jax.experimental import pallas as pl
from jax.experimental.pallas import tpu as pltpu
from jax.sharding import PartitionSpec as P

NX = 96
NY = 192
NZ = 96
MX = 16
MY = 32
MZ = 8
CHANS = 4
CELLS = 6
N_SPACE = 16
N_BLK = 32
PAIR = 2
N_LINE = N_BLK // PAIR
QS = MY // PAIR
ROWS = 16
USED = CHANS // 2 * CELLS
STEP = 4
PARTS = USED // STEP
LANES = 128
HALF = LANES // 2
MODES = PAIR * 2 * MZ
FORWARD = 1.0 / math.sqrt(NX * NY * NZ)
SYNTH = 1.0 / math.sqrt(MX * MY * MZ)
VMEM_LIMIT = 48 * 1024 * 1024
FIRST_X = 2
FIRST_Z = 5
LAST_X = 2
LAST_Z = 5
THERE_LINE = 9
BACK_LINE = 9
F32 = jnp.float32
BF16 = jnp.bfloat16


def members(lead_x, lead_z):
    ring = [((lead_x + x) % 4, (lead_z + z) % 8) for x in range(4) for z in range(8)]
    return [(z % 2, 4 * x + z // 2) for x, z in ring]


FIRST = members(FIRST_X, FIRST_Z)
LAST = members(LAST_X, LAST_Z)


def freqs(count):
    index = np.arange(count)
    return np.where(index < count // 2, index, index - count)


def phases(frequencies, length):
    product = (frequencies[:, None] * np.arange(length)[None, :]) % length
    angles = product.astype(np.float32) * np.float32(2.0 * math.pi / length)
    return np.cos(angles).astype(np.float32), np.sin(angles).astype(np.float32)


def bf16(table):
    return jnp.asarray(table.astype(BF16))


def y_analysis():
    cosines, sines = (v.T.reshape(NY, PAIR, 1, QS) for v in phases(freqs(MY), NY))
    table = np.zeros((2, NY, PAIR, 2, 2, QS), np.float32)
    table[0, :, :, :, 0] = cosines
    table[0, :, :, :, 1] = -sines
    table[1, :, :, :, 0] = -sines
    table[1, :, :, :, 1] = -cosines
    return bf16(table.reshape(2, NY, LANES))


def x_analysis():
    cosines, sines = phases(freqs(MX), NX)
    return bf16(np.concatenate([cosines, sines], 0))


def z_table(order):
    cosines, sines = (v.reshape(MZ, N_SPACE, CELLS) for v in phases(np.arange(MZ), NZ))
    table = np.zeros((2, PAIR, 2, MZ, PAIR, N_SPACE, USED), np.float32)
    for pair in range(PAIR):
        for cl in range(2):
            cells = slice(cl * CELLS, (cl + 1) * CELLS)
            table[0, pair, cl, :, pair, :, cells] = cosines
            table[1, pair, cl, :, pair, :, cells] = sines
    table = table.reshape(2 * MODES, PAIR * N_SPACE, USED)[:, [pair * N_SPACE + space for pair, space in order]]
    return table.reshape(2 * MODES, PAIR * N_SPACE * USED)


def x_synthesis():
    cosines, sines = phases(freqs(MX), NX)
    return bf16(np.concatenate([cosines.T, sines.T], 1))


def y_synthesis():
    cosines, sines = (v.reshape(PAIR, QS, NY) for v in phases(freqs(MY), NY))
    table = np.zeros((2, PAIR, 2, 2, QS, NY), np.float32)
    for h in range(2):
        table[h, :, h, 0] = cosines
        table[h, :, h, 1] = -sines
    return bf16(table.reshape(2, LANES, NY))


def dot(a, b):
    return jnp.dot(a, b, preferred_element_type=F32)


def dot_first(a, b):
    return lax.dot_general(a, b, (((0,), (0,)), ((), ())), preferred_element_type=F32)


def dot_last(a, b):
    return lax.dot_general(a, b, (((1,), (1,)), ((), ())), preferred_element_type=F32)


def index(shape, dim):
    return lax.broadcasted_iota(jnp.int32, shape, dim)


def times_minus_i(a):
    real = index(a.shape, 1) // QS % 2 == 0
    return jnp.where(real, pltpu.roll(a, LANES - QS, 1), -pltpu.roll(a, QS, 1))


def times_i(a):
    real = index(a.shape, 1) // QS % 2 == 0
    return jnp.where(real, -pltpu.roll(a, LANES - QS, 1), pltpu.roll(a, QS, 1))


def low_halves(a, b):
    return jnp.where(index(a.shape, 1) < HALF, a, pltpu.roll(b, HALF, 1))


def high_halves(a, b):
    return jnp.where(index(a.shape, 1) < HALF, pltpu.roll(a, HALF, 1), b)


def analyse_kernel(f_hbm, g_hbm, y_hbm, x_hbm, out_ref, f_ref, g_ref, y_ref, x_ref, sums, planes, sems):
    copies = [pltpu.make_async_copy(x_hbm, x_ref, sems.at[1])]
    for c in range(CHANS):
        copies.append(pltpu.make_async_copy(f_hbm.at[c], f_ref.at[c], sems.at[2 + 2 * c]))
        copies.append(pltpu.make_async_copy(g_hbm.at[c], g_ref.at[c], sems.at[3 + 2 * c]))
    copies.append(pltpu.make_async_copy(y_hbm, y_ref, sems.at[0]))
    for copy in copies:
        copy.start()
    copies[0].wait()
    for c in range(CHANS):
        copies[1 + 2 * c].wait()
        copies[2 + 2 * c].wait()
        for z in range(CELLS):
            for h, v in enumerate((f_ref, g_ref)):
                part = dot(x_ref[...], v[c, z]).astype(BF16)
                start = ((h * CHANS + c) * CELLS + z) * MX
                for r in range(2):
                    sums[r, start : start + MX, :] = part[r * MX : (r + 1) * MX]
    copies[-1].wait()
    both = dot(sums[0], y_ref[0]) + dot(sums[1], y_ref[1])
    half = 2 * USED * MX
    total = jnp.where(index((half, LANES), 1) // (2 * QS) % 2 == 0, both[:half], both[half:])
    for ch in range(2):
        start = ch * ROWS * MX
        planes[start : start + USED * MX, :] = total[ch * USED * MX : (ch + 1) * USED * MX]
    for p in range(MX):
        for part in range(PARTS):
            first = planes[pl.ds(part * STEP * MX + p, STEP, stride=MX), :]
            second = planes[pl.ds((ROWS + part * STEP) * MX + p, STEP, stride=MX), :]
            out_ref[FIRST.index((0, p)), part] = low_halves(first, second).astype(BF16)
            out_ref[FIRST.index((1, p)), part] = high_halves(first, second).astype(BF16)


def in_hbm(values):
    return pltpu.with_memory_space_constraint(values, pltpu.HBM)


def message():
    return jax.ShapeDtypeStruct((PAIR * N_SPACE, PARTS, STEP, LANES), BF16)


def small_message():
    return jax.ShapeDtypeStruct((N_LINE, 2, LANES), BF16)


def line_rows():
    return pltpu.VMEM((2 * N_LINE, LANES), F32)


def put_lines(out_ref, values):
    for place in range(N_LINE):
        out_ref[place] = values[2 * place : 2 * place + 2].astype(BF16)


def take_lines(in_ref, rows):
    for place in range(N_LINE):
        rows[2 * place : 2 * place + 2, :] = in_ref[place].astype(F32)
    return rows[...].astype(BF16)


def field_buffer():
    return pltpu.VMEM((CHANS, CELLS, NX, NY), BF16)


def call(kernel, name, out_shape, *operands, in_specs=None, out_specs=None, scratch=()):
    whole = pl.BlockSpec(memory_space=pltpu.VMEM)
    return pl.pallas_call(
        kernel,
        in_specs=in_specs or [whole] * len(operands),
        out_specs=out_specs or jax.tree.map(lambda _: whole, out_shape),
        out_shape=out_shape,
        scratch_shapes=list(scratch),
        compiler_params=pltpu.CompilerParams(vmem_limit_bytes=VMEM_LIMIT),
        name=name,
    )(*operands)


def analyse(field, cotangent):
    return call(
        analyse_kernel,
        "analyse",
        message(),
        *(in_hbm(v) for v in (field, cotangent, y_analysis(), x_analysis())),
        in_specs=[pl.BlockSpec(memory_space=pltpu.HBM)] * 4,
        scratch=[
            field_buffer(),
            field_buffer(),
            pltpu.VMEM((2, NY, LANES), BF16),
            pltpu.VMEM((2 * MX, NX), BF16),
            pltpu.VMEM((2, 2 * CHANS * CELLS * MX, NY), BF16),
            pltpu.VMEM((2 * ROWS * MX, LANES), F32),
            pltpu.SemaphoreType.DMA((2 + 2 * CHANS,)),
        ],
    )


def line_place(line, lead):
    return (line + N_LINE - lead) % N_LINE


def mode_picker(ch, lead):
    shape = (2 * QS, LANES)
    row, lane = index(shape, 0), index(shape, 1)
    return jnp.where(row == line_place(lane % QS, lead) * 2 + ch, 1.0, 0.0).astype(BF16)


def channel_picker(lead):
    shape = (2 * N_LINE, LANES)
    row, lane = index(shape, 0), index(shape, 1)
    return jnp.where(row == line_place(lane // 4 % N_LINE, lead) * 2 + lane // 2 % 2, 1.0, 0.0).astype(BF16)


def channel_part(shape):
    lane = index(shape, len(shape) - 1)
    return lane // HALF * 2 + lane % 2


def sum_z_kernel(planes_ref, z_ref, out_ref, planes):
    for place in range(PAIR * N_SPACE):
        for part in range(PARTS):
            start = place * USED + part * STEP
            planes[start : start + STEP, :] = planes_ref[place, part].astype(F32)
    sums = dot(z_ref[...], planes[...].astype(BF16))
    spec = sums[:MODES] + times_minus_i(sums[MODES:])
    field = index(spec.shape, 1) // (2 * QS) % 2
    zero = index(spec.shape, 0) % MZ == 0
    scale = jnp.where(field == 0, FORWARD, jnp.where(zero, SYNTH, 2.0 * SYNTH))
    spec = (spec * scale.astype(F32)).astype(BF16).astype(F32)
    shape = (8, MODES, LANES)
    spread = jnp.where(index(shape, 2) // QS == index(shape, 0), spec[None], 0.0).astype(BF16)
    spread = spread.reshape(8 * MODES, LANES)
    first, second = spread[:LANES], spread[LANES:]
    put_lines(out_ref, dot_last(mode_picker(0, THERE_LINE), first) + dot_last(mode_picker(1, THERE_LINE), second))


def mix_kernel(spec_ref, w_ref, back_ref, chan_ref, rows):
    wide = dot_first(take_lines(spec_ref, rows), channel_picker(THERE_LINE)).reshape(4, 4, MZ, LANES)
    part = channel_part((4, MZ, LANES))
    spec = wide[:, 0]
    for j in range(1, 4):
        spec = jnp.where(part == j, wide[:, j], spec)
    chan_ref[...] = spec.reshape(4 * MZ, LANES)
    fr, fi, gr, gi = (spec[i] for i in range(4))
    f = jnp.concatenate([fr, fi], 0).astype(BF16)
    g = jnp.concatenate([gr, gi], 0).astype(BF16)
    own = index((2 * MZ, 2 * LANES), 0) % MZ
    by_f = jnp.zeros((2 * MZ, 2 * LANES), F32)
    by_g = jnp.zeros((2 * MZ, 2 * LANES), F32)
    for k in range(MZ):
        both = w_ref[0, 0, k]
        by_f = jnp.where(own == k, dot_last(f, both.reshape(2 * LANES, LANES)), by_f)
        by_g = jnp.where(own == k, dot(g, jnp.concatenate([both[0], both[1]], 1)), by_g)
    mixed_real = by_f[:MZ, :LANES] - by_f[MZ:, LANES:]
    mixed_imag = by_f[MZ:, :LANES] + by_f[:MZ, LANES:]
    grad_real = by_g[:MZ, :LANES] + by_g[MZ:, LANES:]
    grad_imag = by_g[MZ:, :LANES] - by_g[:MZ, LANES:]
    back = jnp.concatenate([mixed_real, mixed_imag, grad_real, grad_imag], 0)
    back = back.reshape(4, 1, MZ, LANES)
    shape = (4, 4, MZ, LANES)
    spread = jnp.where(channel_part(shape) == index(shape, 1), back, 0.0).astype(BF16)
    put_lines(back_ref, dot_last(channel_picker(BACK_LINE), spread.reshape(LANES, LANES)))


def spread_z_kernel(back_ref, z_ref, out_ref, rows):
    back = take_lines(back_ref, rows)
    owner = index((MODES, LANES), 1) // QS
    spec = jnp.zeros((MODES, LANES), F32)
    for ch in range(2):
        wide = dot_first(back, mode_picker(ch, BACK_LINE)).reshape(4, MODES, LANES)
        for part in range(4):
            spec = jnp.where(owner == 4 * ch + part, wide[part], spec)
    field = owner // 2 % 2
    zero = index(spec.shape, 0) % MZ == 0
    spec = jnp.where((field == 0) & ~zero, 2.0 * spec, spec)
    stacked = jnp.concatenate([spec, times_i(spec)], 0).astype(BF16)
    lane = index((1, LANES), 1) // (2 * QS) % 2
    scale = jnp.where(lane == 0, SYNTH, FORWARD).astype(F32)
    zback = dot(z_ref[...], stacked) * scale
    for place in range(PAIR * N_SPACE):
        for part in range(PARTS):
            start = place * USED + part * STEP
            out_ref[place, part] = zback[start : start + STEP].astype(BF16)


def synthesize_kernel(
    zback_ref, chan_ref, x_ref, y_ref, out_hbm, grad_hbm, wgrad_hbm, out_ref, grad_ref, wgrad_ref, planes, mids, sems
):
    copies = []

    def send(source, target):
        copy = pltpu.make_async_copy(source, target, sems.at[len(copies)])
        copy.start()
        copies.append(copy)

    for place, (pair, space) in enumerate(LAST):
        start = (pair * N_SPACE + space) * ROWS
        for part in range(PARTS):
            planes[start + part * STEP : start + (part + 1) * STEP, :] = zback_ref[place, part].astype(F32)
    columns = chan_ref[2 * MZ :, :].T.astype(BF16)
    fr, fi = chan_ref[:MZ, :], chan_ref[MZ : 2 * MZ, :]
    pairs = jnp.concatenate([jnp.concatenate([fr, -fi], 1), jnp.concatenate([fi, fr], 1)], 0)
    own = index(pairs.shape, 0) % MZ

    for k in range(MZ):
        both = dot(columns, jnp.where(own == k, pairs, 0.0).astype(BF16))
        wgrad_ref[k, 0] = both[:, :LANES]
        wgrad_ref[k, 1] = both[:, LANES:]
    send(wgrad_ref, wgrad_hbm.at[0, 0])

    def turned(c, z):
        row = c % 2 * CELLS + z
        first = planes[pl.ds(row, MX, stride=ROWS), :]
        second = planes[pl.ds(MX * ROWS + row, MX, stride=ROWS), :]
        plane = low_halves(first, second) if c < 2 else high_halves(first, second)
        return jnp.concatenate([plane, times_i(plane)], 0).astype(BF16)

    def x_part(c):
        for z in range(0, CELLS, 2):
            stacked = jnp.concatenate([turned(c, z), turned(c, z + 1)], 1)
            both = dot(x_ref[...], stacked).astype(BF16)
            mids[c, z * NX : (z + 1) * NX, :] = both[:, :LANES]
            mids[c, (z + 1) * NX : (z + 2) * NX, :] = both[:, LANES:]

    def y_part(c):
        both = mids[c]
        for i, (buffer, target) in enumerate(((out_ref, out_hbm), (grad_ref, grad_hbm))):
            buffer[c] = dot(both, y_ref[i]).astype(BF16).reshape(CELLS, NX, NY)
            send(buffer.at[c], target.at[c])

    x_part(0)
    for c in range(CHANS):
        if c + 1 < CHANS:
            x_part(c + 1)
        y_part(c)
    for copy in copies:
        copy.wait()


def synthesize(zback, chan):
    shape = jax.ShapeDtypeStruct((CHANS, CELLS, NX, NY), BF16)
    wgrad = (MZ, 2, LANES, LANES)
    return call(
        synthesize_kernel,
        "synthesize",
        (shape, shape, jax.ShapeDtypeStruct((1, 1) + wgrad, F32)),
        zback,
        chan,
        x_synthesis(),
        y_synthesis(),
        out_specs=(pl.BlockSpec(memory_space=pltpu.HBM),) * 3,
        scratch=[
            field_buffer(),
            field_buffer(),
            pltpu.VMEM(wgrad, F32),
            pltpu.VMEM((PAIR * N_SPACE * ROWS, LANES), F32),
            pltpu.VMEM((CHANS, CELLS * NX, LANES), BF16),
            pltpu.SemaphoreType.DMA((2 * CHANS + 1,)),
        ],
    )


def outer(values, order):
    groups = [[(pair * N_LINE + line) * N_SPACE + space for pair, space in order] for line in range(N_LINE)]
    return lax.all_to_all(values, ("blk", "space"), 0, 0, tiled=True, axis_index_groups=groups)


def inner(values, lead):
    lines = [(lead + place) % N_LINE for place in range(N_LINE)]
    groups = [[pair * N_LINE + line for line in lines] for pair in range(PAIR)]
    return lax.all_to_all(values, "blk", 0, 0, tiled=True, axis_index_groups=groups)


def sum_z(planes):
    return call(sum_z_kernel, "sum_z", small_message(), planes, bf16(z_table(FIRST)), scratch=[pltpu.VMEM((PAIR * N_SPACE * USED, LANES), F32)])


def mix(spec, weights):
    channels = jax.ShapeDtypeStruct((4 * MZ, LANES), F32)
    return call(mix_kernel, "mix", (small_message(), channels), spec, weights, scratch=[line_rows()])


def spread_z(back):
    return call(spread_z_kernel, "spread_z", message(), back, bf16(z_table(LAST).T), scratch=[line_rows()])


def shards(input_field, cotangent, weights):
    planes = outer(analyse(input_field, cotangent), FIRST)
    spec = inner(sum_z(planes), THERE_LINE)
    back, chan = mix(spec, weights)
    back = inner(back, BACK_LINE)
    zback = outer(spread_z(back), LAST)
    return synthesize(zback, chan)


def solution(mesh):
    fields = P("blk", "space", None, None)
    modes = P("space", "blk", None, None, None, None)
    return jax.shard_map(
        shards,
        mesh=mesh,
        in_specs=(fields, fields, modes),
        out_specs=(fields, fields, modes),
        check_vma=False,
    )
```

```python
import math

import jax
import jax.numpy as jnp
import numpy as np
from jax import lax
from jax.experimental import pallas as pl
from jax.experimental.pallas import tpu as pltpu
from jax.sharding import PartitionSpec as P

NX = 96
NY = 192
NZ = 96
MX = 16
MY = 32
MZ = 8
CHANS = 4
CELLS = 6
N_SPACE = 16
N_BLK = 32
PAIR = 2
N_LINE = N_BLK // PAIR
QS = MY // PAIR
ROWS = 16
USED = CHANS // 2 * CELLS
STEP = 4
PARTS = USED // STEP
LANES = 128
HALF = LANES // 2
MODES = PAIR * 2 * MZ
FORWARD = 1.0 / math.sqrt(NX * NY * NZ)
SYNTH = 1.0 / math.sqrt(MX * MY * MZ)
VMEM_LIMIT = 48 * 1024 * 1024
FIRST_X = 2
FIRST_Z = 5
LAST_X = 2
LAST_Z = 5
THERE_LINE = 9
BACK_LINE = 9
F32 = jnp.float32
BF16 = jnp.bfloat16


def members(lead_x, lead_z):
    ring = [((lead_x + x) % 4, (lead_z + z) % 8) for x in range(4) for z in range(8)]
    return [(z % 2, 4 * x + z // 2) for x, z in ring]


FIRST = members(FIRST_X, FIRST_Z)
LAST = members(LAST_X, LAST_Z)


def freqs(count):
    index = np.arange(count)
    return np.where(index < count // 2, index, index - count)


def phases(frequencies, length):
    product = (frequencies[:, None] * np.arange(length)[None, :]) % length
    angles = product.astype(np.float32) * np.float32(2.0 * math.pi / length)
    return np.cos(angles).astype(np.float32), np.sin(angles).astype(np.float32)


def bf16(table):
    return jnp.asarray(table.astype(BF16))


def y_analysis():
    cosines, sines = (v.T.reshape(NY, PAIR, 1, QS) for v in phases(freqs(MY), NY))
    table = np.zeros((2, NY, PAIR, 2, 2, QS), np.float32)
    table[0, :, :, :, 0] = cosines
    table[0, :, :, :, 1] = -sines
    table[1, :, :, :, 0] = -sines
    table[1, :, :, :, 1] = -cosines
    return bf16(table.reshape(2, NY, LANES))


def x_analysis():
    cosines, sines = phases(freqs(MX), NX)
    return bf16(np.concatenate([cosines, sines], 0))


def z_table(order):
    cosines, sines = (v.reshape(MZ, N_SPACE, CELLS) for v in phases(np.arange(MZ), NZ))
    table = np.zeros((2, PAIR, 2, MZ, PAIR, N_SPACE, USED), np.float32)
    for pair in range(PAIR):
        for cl in range(2):
            cells = slice(cl * CELLS, (cl + 1) * CELLS)
            table[0, pair, cl, :, pair, :, cells] = cosines
            table[1, pair, cl, :, pair, :, cells] = sines
    table = table.reshape(2 * MODES, PAIR * N_SPACE, USED)[:, [pair * N_SPACE + space for pair, space in order]]
    return table.reshape(2 * MODES, PAIR * N_SPACE * USED)


def x_synthesis():
    cosines, sines = phases(freqs(MX), NX)
    return bf16(np.concatenate([cosines.T, sines.T], 1))


def y_synthesis():
    cosines, sines = (v.reshape(PAIR, QS, NY) for v in phases(freqs(MY), NY))
    table = np.zeros((2, PAIR, 2, 2, QS, NY), np.float32)
    for h in range(2):
        table[h, :, h, 0] = cosines
        table[h, :, h, 1] = -sines
    return bf16(table.reshape(2, LANES, NY))


def dot(a, b):
    return jnp.dot(a, b, preferred_element_type=F32)


def dot_first(a, b):
    return lax.dot_general(a, b, (((0,), (0,)), ((), ())), preferred_element_type=F32)


def dot_last(a, b):
    return lax.dot_general(a, b, (((1,), (1,)), ((), ())), preferred_element_type=F32)


def index(shape, dim):
    return lax.broadcasted_iota(jnp.int32, shape, dim)


def times_minus_i(a):
    real = index(a.shape, 1) // QS % 2 == 0
    return jnp.where(real, pltpu.roll(a, LANES - QS, 1), -pltpu.roll(a, QS, 1))


def times_i(a):
    real = index(a.shape, 1) // QS % 2 == 0
    return jnp.where(real, -pltpu.roll(a, LANES - QS, 1), pltpu.roll(a, QS, 1))


def low_halves(a, b):
    return jnp.where(index(a.shape, 1) < HALF, a, pltpu.roll(b, HALF, 1))


def high_halves(a, b):
    return jnp.where(index(a.shape, 1) < HALF, pltpu.roll(a, HALF, 1), b)


def analyse_kernel(f_hbm, g_hbm, y_hbm, x_hbm, out_ref, f_ref, g_ref, y_ref, x_ref, sums, planes, sems):
    copies = [pltpu.make_async_copy(x_hbm, x_ref, sems.at[1])]
    for c in range(CHANS):
        copies.append(pltpu.make_async_copy(f_hbm.at[c], f_ref.at[c], sems.at[2 + 2 * c]))
        copies.append(pltpu.make_async_copy(g_hbm.at[c], g_ref.at[c], sems.at[3 + 2 * c]))
    copies.append(pltpu.make_async_copy(y_hbm, y_ref, sems.at[0]))
    for copy in copies:
        copy.start()
    copies[0].wait()
    for c in range(CHANS):
        copies[1 + 2 * c].wait()
        copies[2 + 2 * c].wait()
        for z in range(CELLS):
            for h, v in enumerate((f_ref, g_ref)):
                part = dot(x_ref[...], v[c, z]).astype(BF16)
                start = ((h * CHANS + c) * CELLS + z) * MX
                for r in range(2):
                    sums[r, start : start + MX, :] = part[r * MX : (r + 1) * MX]
    copies[-1].wait()
    both = dot(sums[0], y_ref[0]) + dot(sums[1], y_ref[1])
    half = 2 * USED * MX
    total = jnp.where(index((half, LANES), 1) // (2 * QS) % 2 == 0, both[:half], both[half:])
    for ch in range(2):
        start = ch * ROWS * MX
        planes[start : start + USED * MX, :] = total[ch * USED * MX : (ch + 1) * USED * MX]
    for p in range(MX):
        first = planes[pl.ds(p, USED, stride=MX), :]
        second = planes[pl.ds(ROWS * MX + p, USED, stride=MX), :]
        for pair, chosen in enumerate((low_halves(first, second), high_halves(first, second))):
            for part in range(PARTS):
                out_ref[FIRST.index((pair, p)), part] = chosen[part * STEP : (part + 1) * STEP].astype(BF16)


def in_hbm(values):
    return pltpu.with_memory_space_constraint(values, pltpu.HBM)


def message():
    return jax.ShapeDtypeStruct((PAIR * N_SPACE, PARTS, STEP, LANES), BF16)


def small_message():
    return jax.ShapeDtypeStruct((N_LINE, 2, LANES), BF16)


def line_rows():
    return pltpu.VMEM((2 * N_LINE, LANES), F32)


def put_lines(out_ref, values):
    for place in range(N_LINE):
        out_ref[place] = values[2 * place : 2 * place + 2].astype(BF16)


def take_lines(in_ref, rows):
    for place in range(N_LINE):
        rows[2 * place : 2 * place + 2, :] = in_ref[place].astype(F32)
    return rows[...].astype(BF16)


def field_buffer():
    return pltpu.VMEM((CHANS, CELLS, NX, NY), BF16)


def call(kernel, name, out_shape, *operands, in_specs=None, out_specs=None, scratch=()):
    whole = pl.BlockSpec(memory_space=pltpu.VMEM)
    return pl.pallas_call(
        kernel,
        in_specs=in_specs or [whole] * len(operands),
        out_specs=out_specs or jax.tree.map(lambda _: whole, out_shape),
        out_shape=out_shape,
        scratch_shapes=list(scratch),
        compiler_params=pltpu.CompilerParams(vmem_limit_bytes=VMEM_LIMIT),
        name=name,
    )(*operands)


def analyse(field, cotangent):
    return call(
        analyse_kernel,
        "analyse",
        message(),
        *(in_hbm(v) for v in (field, cotangent, y_analysis(), x_analysis())),
        in_specs=[pl.BlockSpec(memory_space=pltpu.HBM)] * 4,
        scratch=[
            field_buffer(),
            field_buffer(),
            pltpu.VMEM((2, NY, LANES), BF16),
            pltpu.VMEM((2 * MX, NX), BF16),
            pltpu.VMEM((2, 2 * CHANS * CELLS * MX, NY), BF16),
            pltpu.VMEM((2 * ROWS * MX, LANES), F32),
            pltpu.SemaphoreType.DMA((2 + 2 * CHANS,)),
        ],
    )


def line_place(line, lead):
    return (line + N_LINE - lead) % N_LINE


def mode_picker(ch, lead):
    shape = (2 * QS, LANES)
    row, lane = index(shape, 0), index(shape, 1)
    return jnp.where(row == line_place(lane % QS, lead) * 2 + ch, 1.0, 0.0).astype(BF16)


def channel_picker(lead):
    shape = (2 * N_LINE, LANES)
    row, lane = index(shape, 0), index(shape, 1)
    return jnp.where(row == line_place(lane // 4 % N_LINE, lead) * 2 + lane // 2 % 2, 1.0, 0.0).astype(BF16)


def channel_part(shape):
    lane = index(shape, len(shape) - 1)
    return lane // HALF * 2 + lane % 2


def sum_z_kernel(planes_ref, z_ref, out_ref, planes):
    for place in range(PAIR * N_SPACE):
        for part in range(PARTS):
            start = place * USED + part * STEP
            planes[start : start + STEP, :] = planes_ref[place, part].astype(F32)
    sums = dot(z_ref[...], planes[...].astype(BF16))
    spec = sums[:MODES] + times_minus_i(sums[MODES:])
    field = index(spec.shape, 1) // (2 * QS) % 2
    zero = index(spec.shape, 0) % MZ == 0
    scale = jnp.where(field == 0, FORWARD, jnp.where(zero, SYNTH, 2.0 * SYNTH))
    spec = (spec * scale.astype(F32)).astype(BF16).astype(F32)
    shape = (8, MODES, LANES)
    spread = jnp.where(index(shape, 2) // QS == index(shape, 0), spec[None], 0.0).astype(BF16)
    spread = spread.reshape(8 * MODES, LANES)
    first, second = spread[:LANES], spread[LANES:]
    put_lines(out_ref, dot_last(mode_picker(0, THERE_LINE), first) + dot_last(mode_picker(1, THERE_LINE), second))


def mix_kernel(spec_ref, w_ref, back_ref, chan_ref, rows):
    wide = dot_first(take_lines(spec_ref, rows), channel_picker(THERE_LINE)).reshape(4, 4, MZ, LANES)
    part = channel_part((4, MZ, LANES))
    spec = wide[:, 0]
    for j in range(1, 4):
        spec = jnp.where(part == j, wide[:, j], spec)
    chan_ref[...] = spec.reshape(4 * MZ, LANES)
    fr, fi, gr, gi = (spec[i] for i in range(4))
    f = jnp.concatenate([fr, fi], 0).astype(BF16)
    g = jnp.concatenate([gr, gi], 0).astype(BF16)
    own = index((2 * MZ, 2 * LANES), 0) % MZ
    by_f = jnp.zeros((2 * MZ, 2 * LANES), F32)
    by_g = jnp.zeros((2 * MZ, 2 * LANES), F32)
    for k in range(MZ):
        both = w_ref[0, 0, k]
        by_f = jnp.where(own == k, dot_last(f, both.reshape(2 * LANES, LANES)), by_f)
        by_g = jnp.where(own == k, dot(g, jnp.concatenate([both[0], both[1]], 1)), by_g)
    mixed_real = by_f[:MZ, :LANES] - by_f[MZ:, LANES:]
    mixed_imag = by_f[MZ:, :LANES] + by_f[:MZ, LANES:]
    grad_real = by_g[:MZ, :LANES] + by_g[MZ:, LANES:]
    grad_imag = by_g[MZ:, :LANES] - by_g[:MZ, LANES:]
    back = jnp.concatenate([mixed_real, mixed_imag, grad_real, grad_imag], 0)
    back = back.reshape(4, 1, MZ, LANES)
    shape = (4, 4, MZ, LANES)
    spread = jnp.where(channel_part(shape) == index(shape, 1), back, 0.0).astype(BF16)
    put_lines(back_ref, dot_last(channel_picker(BACK_LINE), spread.reshape(LANES, LANES)))


def spread_z_kernel(back_ref, z_ref, out_ref, rows):
    back = take_lines(back_ref, rows)
    owner = index((MODES, LANES), 1) // QS
    spec = jnp.zeros((MODES, LANES), F32)
    for ch in range(2):
        wide = dot_first(back, mode_picker(ch, BACK_LINE)).reshape(4, MODES, LANES)
        for part in range(4):
            spec = jnp.where(owner == 4 * ch + part, wide[part], spec)
    field = owner // 2 % 2
    zero = index(spec.shape, 0) % MZ == 0
    spec = jnp.where((field == 0) & ~zero, 2.0 * spec, spec)
    stacked = jnp.concatenate([spec, times_i(spec)], 0).astype(BF16)
    lane = index((1, LANES), 1) // (2 * QS) % 2
    scale = jnp.where(lane == 0, SYNTH, FORWARD).astype(F32)
    zback = dot(z_ref[...], stacked) * scale
    for place in range(PAIR * N_SPACE):
        for part in range(PARTS):
            start = place * USED + part * STEP
            out_ref[place, part] = zback[start : start + STEP].astype(BF16)


def synthesize_kernel(
    zback_ref, chan_ref, x_ref, y_ref, out_hbm, grad_hbm, wgrad_hbm, out_ref, grad_ref, wgrad_ref, planes, mids, sems
):
    copies = []

    def send(source, target):
        copy = pltpu.make_async_copy(source, target, sems.at[len(copies)])
        copy.start()
        copies.append(copy)

    for place, (pair, space) in enumerate(LAST):
        start = (pair * N_SPACE + space) * ROWS
        for part in range(PARTS):
            planes[start + part * STEP : start + (part + 1) * STEP, :] = zback_ref[place, part].astype(F32)
    columns = chan_ref[2 * MZ :, :].T.astype(BF16)
    fr, fi = chan_ref[:MZ, :], chan_ref[MZ : 2 * MZ, :]
    pairs = jnp.concatenate([jnp.concatenate([fr, -fi], 1), jnp.concatenate([fi, fr], 1)], 0)
    own = index(pairs.shape, 0) % MZ

    for k in range(MZ):
        both = dot(columns, jnp.where(own == k, pairs, 0.0).astype(BF16))
        wgrad_ref[k, 0] = both[:, :LANES]
        wgrad_ref[k, 1] = both[:, LANES:]
    send(wgrad_ref, wgrad_hbm.at[0, 0])

    def turned(c, z):
        row = c % 2 * CELLS + z
        first = planes[pl.ds(row, MX, stride=ROWS), :]
        second = planes[pl.ds(MX * ROWS + row, MX, stride=ROWS), :]
        plane = low_halves(first, second) if c < 2 else high_halves(first, second)
        return jnp.concatenate([plane, times_i(plane)], 0).astype(BF16)

    def x_part(c):
        for z in range(0, CELLS, 2):
            stacked = jnp.concatenate([turned(c, z), turned(c, z + 1)], 1)
            both = dot(x_ref[...], stacked).astype(BF16)
            mids[c, z * NX : (z + 1) * NX, :] = both[:, :LANES]
            mids[c, (z + 1) * NX : (z + 2) * NX, :] = both[:, LANES:]

    def y_part(c):
        both = mids[c]
        for i, (buffer, target) in enumerate(((out_ref, out_hbm), (grad_ref, grad_hbm))):
            buffer[c] = dot(both, y_ref[i]).astype(BF16).reshape(CELLS, NX, NY)
            send(buffer.at[c], target.at[c])

    x_part(0)
    for c in range(CHANS):
        if c + 1 < CHANS:
            x_part(c + 1)
        y_part(c)
    for copy in copies:
        copy.wait()


def synthesize(zback, chan):
    shape = jax.ShapeDtypeStruct((CHANS, CELLS, NX, NY), BF16)
    wgrad = (MZ, 2, LANES, LANES)
    return call(
        synthesize_kernel,
        "synthesize",
        (shape, shape, jax.ShapeDtypeStruct((1, 1) + wgrad, F32)),
        zback,
        chan,
        x_synthesis(),
        y_synthesis(),
        out_specs=(pl.BlockSpec(memory_space=pltpu.HBM),) * 3,
        scratch=[
            field_buffer(),
            field_buffer(),
            pltpu.VMEM(wgrad, F32),
            pltpu.VMEM((PAIR * N_SPACE * ROWS, LANES), F32),
            pltpu.VMEM((CHANS, CELLS * NX, LANES), BF16),
            pltpu.SemaphoreType.DMA((2 * CHANS + 1,)),
        ],
    )


def outer(values, order):
    groups = [[(pair * N_LINE + line) * N_SPACE + space for pair, space in order] for line in range(N_LINE)]
    return lax.all_to_all(values, ("blk", "space"), 0, 0, tiled=True, axis_index_groups=groups)


def inner(values, lead):
    lines = [(lead + place) % N_LINE for place in range(N_LINE)]
    groups = [[pair * N_LINE + line for line in lines] for pair in range(PAIR)]
    return lax.all_to_all(values, "blk", 0, 0, tiled=True, axis_index_groups=groups)


def sum_z(planes):
    return call(sum_z_kernel, "sum_z", small_message(), planes, bf16(z_table(FIRST)), scratch=[pltpu.VMEM((PAIR * N_SPACE * USED, LANES), F32)])


def mix(spec, weights):
    channels = jax.ShapeDtypeStruct((4 * MZ, LANES), F32)
    return call(mix_kernel, "mix", (small_message(), channels), spec, weights, scratch=[line_rows()])


def spread_z(back):
    return call(spread_z_kernel, "spread_z", message(), back, bf16(z_table(LAST).T), scratch=[line_rows()])


def shards(input_field, cotangent, weights):
    planes = outer(analyse(input_field, cotangent), FIRST)
    spec = inner(sum_z(planes), THERE_LINE)
    back, chan = mix(spec, weights)
    back = inner(back, BACK_LINE)
    zback = outer(spread_z(back), LAST)
    return synthesize(zback, chan)


def solution(mesh):
    fields = P("blk", "space", None, None)
    modes = P("space", "blk", None, None, None, None)
    return jax.shard_map(
        shards,
        mesh=mesh,
        in_specs=(fields, fields, modes),
        out_specs=(fields, fields, modes),
        check_vma=False,
    )
```
